32 devices in a mesh: ctx: 32 (over z, y, x, core), head: 1.
Axes of the slice: x: 2, y: 2, z: 4, core: 2. Of those that a mesh axis runs over, the one named last changes fastest.
Arguments:
- shared_qk: bfloat16 [4096, 2048], P('ctx', 'head'), may hold values from -6 to 6
- values: bfloat16 [4096, 2048], P('ctx', 'head'), may hold values from -12 to 12
- out_grad: bfloat16 [4096, 2048], P('ctx', 'head'), may hold values from -6 to 6
- out_weight: bfloat16 [2048, 2048], P('ctx', 'head'), may hold values from -0.125 to 0.125
- buckets: int32 [2, 4096], P(None, 'ctx'), may hold values from 0 to 31, as said below
Outputs:
- mixed: bfloat16 [4096, 2048], P('ctx', 'head')
- grad_qk: bfloat16 [4096, 2048], P('ctx', 'head')
- grad_values: bfloat16 [4096, 2048], P('ctx', 'head')
- grad_weight: float32 [2048, 2048], P('ctx', 'head')
The draws below stay inside these ranges and needn't reach their ends.
Inputs may be any that keep to these rules, and one draw needn't show every extreme that they name: `buckets`: in each round at most 8 of the tokens of one device share a bucket, and one bucket takes exactly 8 tokens from every device.
All inputs are finite; a program needn't handle non-finite values.
Results may differ from the reference program's by a relative error of at most 0.012.
The reference program's roundings to bfloat16 on the way count: a program that leaves them out, or rounds other values in their place, can miss the bound.
Values may be sent and summed in bfloat16 or wider, within the bound.
A program may use at most 128 MiB of HBM per device.

```python
import math
import jax
import jax.numpy as jnp
from jax import lax

D = 2048
HEADS = 16
HEAD_DIM = 128
ROUNDS = 2
SPAN = 128
TOK_DEV = 128
TOKENS = 4096
N_CTX = 32


def draw_shared_qk(key, part):
    key = jax.random.fold_in(key, 11)
    sample_rows = 1.4 * jax.random.normal(key, (TOKENS, D), jnp.float32)
    return jnp.clip(sample_rows, -6.0, 6.0).astype(jnp.bfloat16)


def draw_buckets(key, part):
    key = jax.random.fold_in(key, 7)
    owner_count = TOKENS // TOK_DEV
    per_peer = 2 * TOK_DEV // owner_count

    def one_source(source_key, busiest):
        order_key, slot_key = jax.random.split(source_key)
        shuffled = jax.random.permutation(order_key, TOK_DEV)
        spread = jax.random.permutation(slot_key, (owner_count - 1) * per_peer)[:TOK_DEV - per_peer] // per_peer
        spread = (spread + (spread >= busiest).astype(jnp.int32)).astype(jnp.int32)
        assigned = jnp.concatenate([jnp.full((per_peer,), busiest, jnp.int32), spread])
        return jnp.zeros((TOK_DEV,), jnp.int32).at[shuffled].set(assigned)

    def one_round(round_key):
        busy_key, source_root = jax.random.split(round_key)
        busiest = jax.random.randint(busy_key, (), 0, owner_count).astype(jnp.int32)
        source_keys = jax.random.split(source_root, owner_count)
        return jax.vmap(lambda source_key: one_source(source_key, busiest))(source_keys).reshape(TOKENS)
    return jax.vmap(one_round)(jax.random.split(key, ROUNDS)).astype(jnp.int32)


def steps_of(key, shape, shards, low, high):
    def one(dim, parts):
        draws = jax.random.uniform(jax.random.fold_in(jax.random.fold_in(key, 6), dim), (parts,), jnp.float32, low / len(shards), high / len(shards))
        return jnp.repeat(jnp.exp(draws), shape[dim] // parts).reshape((-1,) + (1,) * (len(shape) - dim - 1))

    loudness = one(*shards[0])
    for cut in shards[1:]:
        loudness = loudness * one(*cut)
    return loudness


def normal_values(own_key, shape, scale, limit, shards=(), kind=jnp.bfloat16):
    entries = scale * jax.random.normal(own_key, shape, jnp.float32)
    if shards:
        entries = entries * steps_of(own_key, shape, shards, -0.22, 0.18)
    return jnp.clip(entries, -limit, limit).astype(kind)


def setup_inputs(seed: int = 0) -> dict:
    streams_of = jax.random.split(jax.random.key(seed), 6)
    shared_qk = draw_shared_qk(jax.random.fold_in(streams_of[5], 71), 0)
    values = normal_values(streams_of[1], (TOKENS, D), 2.0, 12.0, ((0, 32),))
    out_grad = normal_values(streams_of[2], (TOKENS, D), 1.0, 6.0, ((0, 32),))
    out_weight = normal_values(streams_of[3], (D, D), D ** -0.5, 0.125, ((0, 32),))
    buckets = draw_buckets(jax.random.fold_in(streams_of[5], 71), 0)
    return dict(shared_qk=shared_qk, values=values, out_grad=out_grad, out_weight=out_weight, buckets=buckets)


self_penalty = 10000.0
masked_score = -1e+30
highest = lax.Precision.HIGHEST

def rounded(matrix):
    return lax.optimization_barrier(matrix.astype(jnp.bfloat16)).astype(jnp.float32)

def with_zero_row(matrix):
    return jnp.concatenate([matrix, jnp.zeros((1,) + matrix.shape[1:], matrix.dtype)], axis=0)

def key_windows(rows):
    row_count = rows.shape[0]
    leading = jnp.zeros((SPAN,) + rows.shape[1:], rows.dtype)
    earlier = jnp.concatenate([leading, rows[:row_count - SPAN]], axis=0)
    shape_out = (row_count // SPAN, SPAN) + rows.shape[1:]
    return jnp.concatenate([earlier.reshape(shape_out), rows.reshape(shape_out)], axis=1)

def fold_windows(stacked):
    current = stacked[:, SPAN:]
    earlier = stacked[:, :SPAN]
    return current + jnp.concatenate([earlier[1:], jnp.zeros_like(earlier[:1])], axis=0)

def span_probs(queries, key_rows, key_live):
    scores = jnp.einsum('qhd,khd->hqk', queries, key_rows, precision=highest) * HEAD_DIM ** (-0.5)
    itself = jnp.arange(2 * SPAN)[None, :] == jnp.arange(SPAN)[:, None] + SPAN
    scores = jnp.where(itself[None], scores - self_penalty, scores)
    scores = jnp.where(key_live[None, None, :], scores, masked_score)
    largest = lax.optimization_barrier(jnp.max(scores, axis=-1, keepdims=True))
    lifted = jnp.exp(scores - largest)
    summed = lax.optimization_barrier(jnp.sum(lifted, axis=-1, keepdims=True))
    return (lifted / summed, (largest + jnp.log(summed))[..., 0])

def owner_forward(own_qk, own_values, occupied):
    head_count = own_qk.shape[1] // HEAD_DIM
    blocks = own_qk.shape[0] // SPAN
    queries = own_qk.reshape(blocks, SPAN, head_count, HEAD_DIM)
    key_rows = key_windows(own_qk).reshape(blocks, 2 * SPAN, head_count, HEAD_DIM)
    value_rows = key_windows(own_values).reshape(blocks, 2 * SPAN, head_count, HEAD_DIM)
    live_keys = key_windows(occupied)

    def one_block(pieces):
        block_query, block_key, block_value, block_live = pieces
        probability, log_total = span_probs(block_query, block_key, block_live)
        result = jnp.einsum('hqk,khd->qhd', rounded(probability), block_value, precision=highest)
        return (rounded(result).reshape(SPAN, head_count * HEAD_DIM), log_total.T)
    outputs, log_totals = lax.map(one_block, (queries, key_rows, value_rows, live_keys))
    return (outputs.reshape(-1, head_count * HEAD_DIM), log_totals.reshape(-1, head_count))

def owner_backward(own_qk, own_values, occupied, own_grad, own_shift):
    head_count = own_qk.shape[1] // HEAD_DIM
    blocks = own_qk.shape[0] // SPAN
    queries = own_qk.reshape(blocks, SPAN, head_count, HEAD_DIM)
    key_rows = key_windows(own_qk).reshape(blocks, 2 * SPAN, head_count, HEAD_DIM)
    value_rows = key_windows(own_values).reshape(blocks, 2 * SPAN, head_count, HEAD_DIM)
    live_keys = key_windows(occupied)
    grad_rows = own_grad.reshape(blocks, SPAN, head_count, HEAD_DIM)
    shift_rows = own_shift.reshape(blocks, SPAN, head_count)

    def one_block(pieces):
        block_query, block_key, block_value, block_live, block_grad, block_shift = pieces
        probability, log_total = span_probs(block_query, block_key, block_live)
        prob_grad = jnp.einsum('qhd,khd->hqk', block_grad, block_value, precision=highest)
        score_grad = rounded(probability * (prob_grad - block_shift.T[:, :, None]))
        query_grad = jnp.einsum('hqk,khd->qhd', score_grad, block_key, precision=highest) * HEAD_DIM ** (-0.5)
        key_grad = jnp.einsum('hqk,qhd->khd', score_grad, block_query, precision=highest) * HEAD_DIM ** (-0.5)
        value_grad = jnp.einsum('hqk,qhd->khd', rounded(probability), block_grad, precision=highest)
        return (query_grad, key_grad, value_grad)
    query_grad, key_grad, value_grad = lax.map(one_block, (queries, key_rows, value_rows, live_keys, grad_rows, shift_rows))
    row_width = head_count * HEAD_DIM
    qk_rows = (query_grad + fold_windows(key_grad)).reshape(-1, row_width).astype(jnp.bfloat16)
    value_out = fold_windows(value_grad).reshape(-1, row_width).astype(jnp.bfloat16)
    return (qk_rows, value_out)

def route_round(bucket_row, capacity):
    owners = jnp.arange(N_CTX, dtype=jnp.int32)
    ordering = jnp.argsort(bucket_row, stable=True).astype(jnp.int32)
    counts = lax.optimization_barrier(jnp.sum((bucket_row[:, None] == owners[None, :]).astype(jnp.int32), axis=0))
    starts = jnp.cumsum(counts) - counts
    offsets = jnp.arange(capacity, dtype=jnp.int32)
    occupied = offsets[None, :] < counts[:, None]
    picked = jnp.minimum(starts[:, None] + offsets[None, :], TOKENS - 1).astype(jnp.int32)
    token_index = jnp.where(occupied, ordering[picked], TOKENS).astype(jnp.int32)
    return (token_index, occupied)

def reference(shared_qk, values, out_grad, out_weight, buckets):
    capacity = 2 * TOK_DEV
    padded_qk = with_zero_row(shared_qk)
    padded_values = with_zero_row(values)
    routes = [route_round(buckets[round_index], capacity) for round_index in range(ROUNDS)]
    round_outputs = []
    round_logs = []
    for round_index in range(ROUNDS):
        token_index, occupied = routes[round_index]

        def owner_step(pieces):
            owner_tokens, owner_live = pieces
            own_qk = padded_qk[owner_tokens].astype(jnp.float32)
            own_values = padded_values[owner_tokens].astype(jnp.float32)
            rows_out, logs_out = owner_forward(own_qk, own_values, owner_live)
            return (rows_out.astype(jnp.bfloat16), logs_out)
        rows_all, logs_all = lax.map(owner_step, (token_index, occupied))
        flat_index = token_index.reshape(-1)
        round_outputs.append(jnp.zeros((TOKENS + 1, D), jnp.bfloat16).at[flat_index].set(rows_all.reshape(-1, D))[:TOKENS])
        round_logs.append(jnp.zeros((TOKENS + 1, HEADS), jnp.float32).at[flat_index].set(logs_all.reshape(-1, HEADS))[:TOKENS])
    log_stack = jnp.stack(round_logs)
    largest = lax.optimization_barrier(jnp.max(log_stack, axis=0))
    lifted = jnp.exp(log_stack - largest)
    round_weight = lifted / lax.optimization_barrier(jnp.sum(lifted, axis=0))
    row_stack = jnp.stack(round_outputs).astype(jnp.float32).reshape(ROUNDS, TOKENS, HEADS, HEAD_DIM)
    attended = lax.optimization_barrier(jnp.sum(round_weight[..., None] * row_stack, axis=0)).reshape(TOKENS, D).astype(jnp.bfloat16)
    mixed = jnp.dot(attended, out_weight.T, preferred_element_type=jnp.float32).astype(jnp.bfloat16)
    attended_grad = jnp.dot(out_grad, out_weight, preferred_element_type=jnp.float32)
    grad_weight = jnp.dot(out_grad.T, attended, preferred_element_type=jnp.float32) * (1.0 / math.sqrt(TOKENS))
    grad_heads = attended_grad.reshape(TOKENS, HEADS, HEAD_DIM)
    inner = lax.optimization_barrier(jnp.sum(grad_heads * attended.astype(jnp.float32).reshape(TOKENS, HEADS, HEAD_DIM), axis=-1))
    qk_total = jnp.zeros((TOKENS, D), jnp.float32)
    value_total = jnp.zeros((TOKENS, D), jnp.float32)
    for round_index in range(ROUNDS):
        token_index, occupied = routes[round_index]
        query_grad = (round_weight[round_index][..., None] * grad_heads).reshape(TOKENS, D).astype(jnp.bfloat16)
        padded_grad = with_zero_row(query_grad)
        padded_shift = with_zero_row(round_weight[round_index] * inner)

        def owner_back(pieces):
            owner_tokens, owner_live = pieces
            own_qk = padded_qk[owner_tokens].astype(jnp.float32)
            own_values = padded_values[owner_tokens].astype(jnp.float32)
            own_grad = padded_grad[owner_tokens].astype(jnp.float32)
            own_shift = padded_shift[owner_tokens]
            return owner_backward(own_qk, own_values, owner_live, own_grad, own_shift)
        qk_all, value_all = lax.map(owner_back, (token_index, occupied))
        flat_index = token_index.reshape(-1)
        qk_total = qk_total + jnp.zeros((TOKENS + 1, D), jnp.bfloat16).at[flat_index].set(qk_all.reshape(-1, D))[:TOKENS].astype(jnp.float32)
        value_total = value_total + jnp.zeros((TOKENS + 1, D), jnp.bfloat16).at[flat_index].set(value_all.reshape(-1, D))[:TOKENS].astype(jnp.float32)
    return (mixed, qk_total.astype(jnp.bfloat16), value_total.astype(jnp.bfloat16), grad_weight)
```

```python
import math

import jax
import jax.numpy as jnp
from jax import lax
from jax.experimental import pallas as pl
from jax.experimental.pallas import tpu as pltpu
from jax.sharding import PartitionSpec as P

HEAD_DIM = 128
SPAN = 128


self_penalty = 10000.0
masked_score = -1e30


def with_zero_row(matrix):
    return jnp.concatenate([matrix, jnp.zeros((1,) + matrix.shape[1:], matrix.dtype)], axis=0)


def key_windows(rows):
    row_count = rows.shape[0]
    leading = jnp.zeros((SPAN,) + rows.shape[1:], rows.dtype)
    earlier = jnp.concatenate([leading, rows[: row_count - SPAN]], axis=0)
    shape_out = (row_count // SPAN, SPAN) + rows.shape[1:]
    return jnp.concatenate([earlier.reshape(shape_out), rows.reshape(shape_out)], axis=1)


def fold_windows(stacked):
    current = stacked[:, SPAN:]
    earlier = stacked[:, :SPAN]
    return current + jnp.concatenate([earlier[1:], jnp.zeros_like(earlier[:1])], axis=0)


def span_probs(queries, key_rows, key_live):
    scores = jnp.einsum(
        "qhd,khd->hqk", queries, key_rows, preferred_element_type=jnp.float32
    ) * HEAD_DIM ** (-0.5)
    itself = jnp.arange(2 * SPAN)[None, :] == jnp.arange(SPAN)[:, None] + SPAN
    scores = jnp.where(itself[None], scores - self_penalty, scores)
    scores = jnp.where(key_live[None, None, :], scores, masked_score)
    largest = jnp.max(scores, axis=-1, keepdims=True)
    lifted = jnp.exp(scores - largest)
    summed = jnp.sum(lifted, axis=-1, keepdims=True)
    return (lifted / summed, (largest + jnp.log(summed))[..., 0])


def owner_forward(own_qk, own_values, occupied, local_heads):
    blocks = own_qk.shape[0] // SPAN
    queries = own_qk.reshape(blocks, SPAN, local_heads, HEAD_DIM)
    key_rows = key_windows(own_qk).reshape(blocks, 2 * SPAN, local_heads, HEAD_DIM)
    value_rows = key_windows(own_values).reshape(blocks, 2 * SPAN, local_heads, HEAD_DIM)
    live_keys = key_windows(occupied)

    def one_block(pieces):
        block_query, block_key, block_value, block_live = pieces
        probability, log_total = span_probs(block_query, block_key, block_live)
        result = jnp.einsum(
            "hqk,khd->qhd",
            probability.astype(jnp.bfloat16),
            block_value,
            preferred_element_type=jnp.float32,
        )
        return (result.astype(jnp.bfloat16).reshape(SPAN, local_heads * HEAD_DIM), log_total.T)

    outputs, log_totals = lax.map(one_block, (queries, key_rows, value_rows, live_keys))
    return (outputs.reshape(-1, local_heads * HEAD_DIM), log_totals.reshape(-1, local_heads))


def owner_backward(own_qk, own_values, occupied, own_grad, own_shift, local_heads):
    blocks = own_qk.shape[0] // SPAN
    queries = own_qk.reshape(blocks, SPAN, local_heads, HEAD_DIM)
    key_rows = key_windows(own_qk).reshape(blocks, 2 * SPAN, local_heads, HEAD_DIM)
    value_rows = key_windows(own_values).reshape(blocks, 2 * SPAN, local_heads, HEAD_DIM)
    live_keys = key_windows(occupied)
    grad_rows = own_grad.reshape(blocks, SPAN, local_heads, HEAD_DIM)
    shift_rows = own_shift.reshape(blocks, SPAN, local_heads)

    def one_block(pieces):
        block_query, block_key, block_value, block_live, block_grad, block_shift = pieces
        probability, log_total = span_probs(block_query, block_key, block_live)
        prob_grad = jnp.einsum(
            "qhd,khd->hqk", block_grad, block_value, preferred_element_type=jnp.float32
        )
        score_grad = (probability * (prob_grad - block_shift.T[:, :, None])).astype(jnp.bfloat16)
        query_grad = jnp.einsum(
            "hqk,khd->qhd", score_grad, block_key, preferred_element_type=jnp.float32
        ) * HEAD_DIM ** (-0.5)
        key_grad = jnp.einsum(
            "hqk,qhd->khd", score_grad, block_query, preferred_element_type=jnp.float32
        ) * HEAD_DIM ** (-0.5)
        value_grad = jnp.einsum(
            "hqk,qhd->khd",
            probability.astype(jnp.bfloat16),
            block_grad,
            preferred_element_type=jnp.float32,
        )
        return (query_grad, key_grad, value_grad)

    query_grad, key_grad, value_grad = lax.map(
        one_block, (queries, key_rows, value_rows, live_keys, grad_rows, shift_rows)
    )
    row_width = local_heads * HEAD_DIM
    qk_rows = (query_grad + fold_windows(key_grad)).reshape(-1, row_width).astype(jnp.bfloat16)
    value_out = fold_windows(value_grad).reshape(-1, row_width).astype(jnp.bfloat16)
    return (qk_rows, value_out)


def route_round(bucket_row, peer_count, per_peer, token_rows):
    owners = jnp.arange(peer_count, dtype=jnp.int32)
    member = (bucket_row[:, None] == owners[None, :]).astype(jnp.int32)
    earlier = jnp.cumsum(member, axis=0) - member
    position = jnp.sum(earlier * member, axis=1)
    slot_index = bucket_row * per_peer + position
    slot_token = (
        jnp.full((peer_count * per_peer,), token_rows, jnp.int32)
        .at[slot_index]
        .set(jnp.arange(token_rows, dtype=jnp.int32))
    )
    return (slot_index, slot_token)


def compact_slots(slot_marks, capacity):
    target = jnp.cumsum(slot_marks) - 1
    target = jnp.where(slot_marks > 0, target, capacity).astype(jnp.int32)
    source_slot = (
        jnp.full((capacity,), capacity, jnp.int32)
        .at[target]
        .set(jnp.arange(capacity, dtype=jnp.int32), mode="drop")
    )
    return (source_slot, target)


def bucket_owner_device(shared_qk, values, out_grad, out_weight, buckets):
    token_rows, row_width = shared_qk.shape
    local_heads = row_width // HEAD_DIM
    peer_count = lax.axis_size("ctx")
    capacity = 2 * token_rows
    per_peer = capacity // peer_count
    rounds = buckets.shape[0]
    routes = [
        route_round(buckets[round_index], peer_count, per_peer, token_rows)
        for round_index in range(rounds)
    ]
    padded_qk = with_zero_row(shared_qk)
    padded_values = with_zero_row(values)
    whole_weight = lax.all_gather(out_weight, "ctx", axis=0, tiled=True)
    groups = [[round_index] for round_index in range(rounds)]

    def outgoing(matrix, round_index):
        return matrix[routes[round_index][1]].reshape((peer_count, per_peer) + matrix.shape[1:])

    def homeward(received, round_index):
        flat_rows = received.reshape((peer_count * per_peer,) + received.shape[2:])
        return flat_rows[routes[round_index][0]]

    round_outputs = [None] * rounds
    round_logs = [None] * rounds
    owner_state = [None] * rounds
    for round_group in groups:
        send_qk = jnp.stack(
            [outgoing(padded_qk, round_index) for round_index in round_group], axis=1
        )
        send_values = jnp.stack(
            [outgoing(padded_values, round_index) for round_index in round_group], axis=1
        )
        slot_marks = jnp.stack(
            [
                (routes[round_index][1] < token_rows)
                .astype(jnp.int32)
                .reshape(peer_count, per_peer)
                for round_index in round_group
            ],
            axis=1,
        )
        got_qk, got_values, got_marks = (
            lax.all_to_all(send_qk, "ctx", split_axis=0, concat_axis=0, tiled=True),
            lax.all_to_all(send_values, "ctx", split_axis=0, concat_axis=0, tiled=True),
            lax.all_to_all(slot_marks, "ctx", split_axis=0, concat_axis=0, tiled=True),
        )
        returned_rows = []
        returned_logs = []
        for member_index, round_index in enumerate(round_group):
            source_slot, target = compact_slots(got_marks[:, member_index].reshape(-1), capacity)
            own_qk = with_zero_row(got_qk[:, member_index].reshape(capacity, row_width))[
                source_slot
            ]
            own_values = with_zero_row(got_values[:, member_index].reshape(capacity, row_width))[
                source_slot
            ]
            occupied = source_slot < capacity
            rows_out, logs_out = owner_forward(own_qk, own_values, occupied, local_heads)
            owner_state[round_index] = (own_qk, own_values, occupied, source_slot, target)
            returned_rows.append(
                with_zero_row(rows_out)[target].reshape(peer_count, per_peer, row_width)
            )
            returned_logs.append(
                with_zero_row(logs_out)[target].reshape(peer_count, per_peer, local_heads)
            )
        back_rows, back_logs = (
            lax.all_to_all(
                jnp.stack(returned_rows, axis=1).astype(jnp.float32),
                "ctx",
                split_axis=0,
                concat_axis=0,
                tiled=True,
            ).astype(jnp.bfloat16),
            lax.all_to_all(
                jnp.stack(returned_logs, axis=1), "ctx", split_axis=0, concat_axis=0, tiled=True
            ),
        )
        for member_index, round_index in enumerate(round_group):
            round_outputs[round_index] = homeward(back_rows[:, member_index], round_index)
            round_logs[round_index] = homeward(back_logs[:, member_index], round_index)
    log_stack = jnp.stack(round_logs)
    largest = jnp.max(log_stack, axis=0)
    lifted = jnp.exp(log_stack - largest)
    round_weight = lifted / jnp.sum(lifted, axis=0)
    row_stack = (
        jnp.stack(round_outputs)
        .astype(jnp.float32)
        .reshape(rounds, token_rows, local_heads, HEAD_DIM)
    )
    attended = (
        jnp.sum(round_weight[..., None] * row_stack, axis=0)
        .reshape(token_rows, row_width)
        .astype(jnp.bfloat16)
    )
    partial_value = lax.dot_general(
        attended, whole_weight, (((1,), (1,)), ((), ())), preferred_element_type=jnp.float32
    )
    mixed = lax.psum_scatter(partial_value, "head", scatter_dimension=1, tiled=True).astype(
        jnp.bfloat16
    )
    full_grad = lax.all_gather(out_grad, "head", axis=1, tiled=True)
    attended_grad = jnp.dot(full_grad, whole_weight, preferred_element_type=jnp.float32)
    token_total = token_rows * peer_count
    grad_weight = lax.psum_scatter(
        lax.dot_general(
            full_grad, attended, (((0,), (0,)), ((), ())), preferred_element_type=jnp.float32
        ),
        "ctx",
        scatter_dimension=0,
        tiled=True,
    ) * (1.0 / math.sqrt(token_total))
    grad_heads = attended_grad.reshape(token_rows, local_heads, HEAD_DIM)
    inner = jnp.sum(
        grad_heads * attended.astype(jnp.float32).reshape(token_rows, local_heads, HEAD_DIM),
        axis=-1,
    )
    qk_total = jnp.zeros((token_rows, row_width), jnp.float32)
    value_total = jnp.zeros((token_rows, row_width), jnp.float32)
    for round_group in groups:
        send_grad = jnp.stack(
            [
                outgoing(
                    with_zero_row(
                        (round_weight[round_index][..., None] * grad_heads)
                        .reshape(token_rows, row_width)
                        .astype(jnp.bfloat16)
                    ),
                    round_index,
                )
                for round_index in round_group
            ],
            axis=1,
        )
        send_shift = jnp.stack(
            [
                outgoing(with_zero_row(round_weight[round_index] * inner), round_index)
                for round_index in round_group
            ],
            axis=1,
        )
        got_grad, got_shift = (
            lax.all_to_all(
                send_grad.astype(jnp.float32), "ctx", split_axis=0, concat_axis=0, tiled=True
            ).astype(send_grad.dtype),
            lax.all_to_all(send_shift, "ctx", split_axis=0, concat_axis=0, tiled=True),
        )
        returned_qk = []
        returned_values = []
        for member_index, round_index in enumerate(round_group):
            own_qk, own_values, occupied, source_slot, target = owner_state[round_index]
            own_grad = with_zero_row(got_grad[:, member_index].reshape(capacity, row_width))[
                source_slot
            ]
            own_shift = with_zero_row(got_shift[:, member_index].reshape(capacity, local_heads))[
                source_slot
            ]
            qk_rows, value_rows = owner_backward(
                own_qk, own_values, occupied, own_grad, own_shift, local_heads
            )
            returned_qk.append(
                with_zero_row(qk_rows)[target].reshape(peer_count, per_peer, row_width)
            )
            returned_values.append(
                with_zero_row(value_rows)[target].reshape(peer_count, per_peer, row_width)
            )
        back_qk, back_values = (
            lax.all_to_all(
                jnp.stack(returned_qk, axis=1), "ctx", split_axis=0, concat_axis=0, tiled=True
            ),
            lax.all_to_all(
                jnp.stack(returned_values, axis=1), "ctx", split_axis=0, concat_axis=0, tiled=True
            ),
        )
        for member_index, round_index in enumerate(round_group):
            qk_total = qk_total + homeward(back_qk[:, member_index], round_index).astype(
                jnp.float32
            )
            value_total = value_total + homeward(back_values[:, member_index], round_index).astype(
                jnp.float32
            )
    return (mixed, qk_total.astype(jnp.bfloat16), value_total.astype(jnp.bfloat16), grad_weight)


PLANES = 4
TALL = 256
VMEM_BYTES = 48 * 1024 * 1024


def contract(left, right, left_dim, right_dim):
    return lax.dot_general(
        left, right, (((left_dim,), (right_dim,)), ((), ())), preferred_element_type=jnp.float32
    )


def slot_pick(slot_ref, source):
    slot_ids = lax.broadcasted_iota(jnp.int32, (TALL, SPAN), 0)
    return (slot_ids == slot_ref[pl.ds(source, 1), :]).astype(jnp.bfloat16)


def bucket_scores(rows, code_ref, bucket):
    scores = contract(rows, rows, 1, 1) * HEAD_DIM ** (-0.5)
    key_ids = lax.broadcasted_iota(jnp.int32, (TALL, TALL), 0)
    query_ids = lax.broadcasted_iota(jnp.int32, (TALL, TALL), 1)
    scores = jnp.where(key_ids == query_ids, scores - self_penalty, scores)
    code_row = code_ref[pl.ds(bucket, 1), :]
    code_column = jnp.broadcast_to(code_row, (SPAN, TALL)).T
    code_column = jnp.concatenate([code_column, code_column], axis=1)
    seen = (code_column > 0.5) & (code_column <= jnp.maximum(code_row, 1.0))
    return jnp.where(seen, scores, masked_score)


def forward_kernel(mine_ref, other_ref, slot_ref, code_ref, out_ref, log_ref, grouped, results):
    sources, slots = grouped.shape[0], grouped.shape[1]
    per_peer = TALL // sources
    buckets = slots // per_peer

    def group(source, carry):
        rows = jnp.concatenate([mine_ref[source], other_ref[source]], axis=0)
        grouped[source] = contract(slot_pick(slot_ref, source), rows, 1, 0)
        return carry

    lax.fori_loop(0, sources, group, 0, unroll=2)

    def attend(bucket, carry):
        place = pl.ds(pl.multiple_of(bucket * per_peer, per_peer), per_peer)
        rows = grouped[:, place, :].reshape(TALL, 2 * HEAD_DIM).astype(jnp.bfloat16)
        scores = bucket_scores(rows[:, :HEAD_DIM], code_ref, bucket)
        largest = jnp.max(scores, axis=0, keepdims=True)
        lifted = jnp.exp(scores - largest)
        summed = jnp.sum(lifted, axis=0, keepdims=True)
        probability = (lifted / summed).astype(jnp.bfloat16)
        result = contract(probability, rows[:, HEAD_DIM:], 0, 0)
        results[:, place, :] = result.reshape(sources, per_peer, HEAD_DIM)
        log_ref[pl.ds(bucket, 1), :] = largest + jnp.log(summed)
        return carry

    lax.fori_loop(0, buckets, attend, 0, unroll=2)

    def scatter(source, carry):
        rows = results[source].astype(jnp.bfloat16)
        out_ref[source] = contract(slot_pick(slot_ref, source), rows, 0, 0).astype(jnp.bfloat16)
        return carry

    lax.fori_loop(0, sources, scatter, 0, unroll=2)


def backward_kernel(
    mine_ref, other_ref, grad_ref, slot_ref, code_ref, log_ref, shift_ref, out_ref, grouped, results
):
    sources, slots = grouped.shape[0], grouped.shape[1]
    per_peer = TALL // sources
    buckets = slots // per_peer
    both = 2 * HEAD_DIM

    def group(source, carry):
        rows = jnp.concatenate([mine_ref[source], other_ref[source]], axis=0)
        pick = slot_pick(slot_ref, source)
        grouped[source, :, :both] = contract(pick, rows, 1, 0)
        grouped[source, :, both:] = contract(pick, grad_ref[source], 1, 0)
        return carry

    lax.fori_loop(0, sources, group, 0, unroll=2)

    def attend(bucket, carry):
        place = pl.ds(pl.multiple_of(bucket * per_peer, per_peer), per_peer)
        rows = grouped[:, place, :].reshape(TALL, 3 * HEAD_DIM).astype(jnp.bfloat16)
        qk_rows, value_rows, grad_rows = (
            rows[:, :HEAD_DIM],
            rows[:, HEAD_DIM:both],
            rows[:, both:],
        )
        scores = bucket_scores(qk_rows, code_ref, bucket)
        probability = jnp.exp(scores - log_ref[pl.ds(bucket, 1), :])
        prob_grad = contract(value_rows, grad_rows, 1, 1)
        score_grad = (probability * (prob_grad - shift_ref[pl.ds(bucket, 1), :])).astype(
            jnp.bfloat16
        )
        qk_grad = contract(score_grad, qk_rows, 0, 0) + contract(score_grad, qk_rows, 1, 0)
        value_grad = contract(probability.astype(jnp.bfloat16), grad_rows, 1, 0)
        results[:, place, :HEAD_DIM] = (qk_grad * HEAD_DIM ** (-0.5)).reshape(
            sources, per_peer, HEAD_DIM
        )
        results[:, place, HEAD_DIM:] = value_grad.reshape(sources, per_peer, HEAD_DIM)
        return carry

    lax.fori_loop(0, buckets, attend, 0, unroll=2)

    def scatter(source, carry):
        rows = results[source].astype(jnp.bfloat16)
        out_ref[source] = contract(slot_pick(slot_ref, source), rows, 0, 0).astype(jnp.bfloat16)
        return carry

    lax.fori_loop(0, sources, scatter, 0, unroll=2)


def kernel_call(body, out_shape, scratch_shapes, arguments):
    return pl.pallas_call(
        body,
        out_shape=out_shape,
        in_specs=[pl.BlockSpec(memory_space=pltpu.VMEM)] * len(arguments),
        out_specs=jax.tree.map(lambda _: pl.BlockSpec(memory_space=pltpu.VMEM), out_shape),
        scratch_shapes=scratch_shapes,
        compiler_params=pltpu.CompilerParams(vmem_limit_bytes=VMEM_BYTES),
    )(*arguments)


def head_owner_device(shared_qk, values, out_grad, out_weight, buckets):
    token_rows, row_width = shared_qk.shape
    heads = row_width // HEAD_DIM
    peers = lax.axis_size("ctx")
    per_peer = 2 * token_rows // peers
    half = token_rows // 2
    slots = peers * per_peer
    core = lax.axis_index("ctx") % 2
    first = core == 0
    partners = [(device, device ^ 1) for device in range(peers)]

    def exchange(block):
        return lax.ppermute(block, "ctx", partners)

    def swapped(block):
        return jnp.concatenate([block[:, half:], block[:, :half]], axis=1)

    def everywhere(block):
        return lax.all_to_all(block, "ctx", split_axis=0, concat_axis=0, tiled=True)

    def by_head(rows):
        return rows.reshape(2, half, heads, HEAD_DIM).transpose(2, 0, 1, 3)

    def by_token(blocks):
        return blocks.reshape(heads, 2, half, HEAD_DIM).transpose(1, 2, 0, 3).reshape(
            token_rows, row_width
        )

    all_buckets = lax.all_gather(buckets, "ctx", axis=0)
    whole_weight = lax.all_gather(out_weight, "ctx", axis=0, tiled=True)

    own = jnp.where(first, all_buckets[:, 0], all_buckets[:, 1])
    order = jnp.arange(token_rows, dtype=jnp.int32)
    same = (own[:, :, None] == own[:, None, :]) & (order[None, :] < order[:, None])[None]
    position = jnp.sum(same.astype(jnp.int32), axis=2)
    slot = own * per_peer + position
    slot = jnp.where(first, slot, swapped(slot))
    bucket_ids = jnp.arange(peers, dtype=jnp.int32)
    counts = jnp.sum((own[:, :, None] == bucket_ids).astype(jnp.int32), axis=1)
    before = (bucket_ids[None, :] < bucket_ids[:, None]).astype(jnp.int32)
    starts = jnp.sum(before[:, :, None] * counts[None], axis=1)
    within = jnp.arange(per_peer, dtype=jnp.int32)
    live = within < counts[:, :, None]
    code = jnp.where(live, jnp.where(starts[:, :, None] + within >= SPAN, 2.0, 1.0), 0.0)
    code = code.astype(jnp.float32).transpose(1, 0, 2).reshape(peers, peers * per_peer)

    sent = jnp.concatenate([by_head(shared_qk), by_head(values)], axis=-1)
    mine = everywhere(sent.reshape(peers, half, 2 * HEAD_DIM))
    other = exchange(mine)

    result, log_slots = kernel_call(
        forward_kernel,
        (
            jax.ShapeDtypeStruct((peers, token_rows, HEAD_DIM), jnp.bfloat16),
            jax.ShapeDtypeStruct((peers, peers * per_peer), jnp.float32),
        ),
        [
            pltpu.VMEM((peers, slots, 2 * HEAD_DIM), jnp.float32),
            pltpu.VMEM((peers, slots, HEAD_DIM), jnp.float32),
        ],
        (mine, other, slot, code),
    )

    attended_grad = jnp.dot(out_grad, whole_weight, preferred_element_type=jnp.float32).astype(
        jnp.bfloat16
    )
    grad_mine = everywhere(by_head(attended_grad).reshape(peers, half, HEAD_DIM))
    grad_rows = jnp.concatenate([grad_mine, exchange(grad_mine)], axis=1).astype(jnp.float32)

    chosen = slot[:, :, None] == jnp.arange(slots, dtype=jnp.int32)
    log_by_source = log_slots.reshape(peers, peers, per_peer).transpose(1, 0, 2).reshape(peers, slots)
    log_own = jnp.sum(jnp.where(chosen, log_by_source[:, None, :], 0.0), axis=2)
    log_other = swapped(exchange(log_own))
    result_other = swapped(exchange(result))
    largest = jnp.maximum(log_own, log_other)
    lifted_own, lifted_other = jnp.exp(log_own - largest), jnp.exp(log_other - largest)
    lifted_sum = lifted_own + lifted_other
    weight_own, weight_other = lifted_own / lifted_sum, lifted_other / lifted_sum
    attended = (
        weight_own[:, :, None] * result.astype(jnp.float32)
        + weight_other[:, :, None] * result_other.astype(jnp.float32)
    ).astype(jnp.bfloat16)

    inner = jnp.sum(grad_rows * attended.astype(jnp.float32), axis=-1)
    shift = weight_own * inner
    query_grad = (weight_own[:, :, None] * grad_rows).astype(jnp.bfloat16)
    shift_slots = jnp.sum(jnp.where(chosen, shift[:, :, None], 0.0), axis=1)
    shift_slots = (
        shift_slots.reshape(peers, peers, per_peer).transpose(1, 0, 2).reshape(peers, slots)
    )

    attended_rows = by_token(everywhere(attended[:, :half]))

    grads = kernel_call(
        backward_kernel,
        jax.ShapeDtypeStruct((peers, token_rows, 2 * HEAD_DIM), jnp.bfloat16),
        [
            pltpu.VMEM((peers, slots, 3 * HEAD_DIM), jnp.float32),
            pltpu.VMEM((peers, slots, 2 * HEAD_DIM), jnp.float32),
        ],
        (mine, other, query_grad, slot, code, log_slots, shift_slots),
    )
    grads_other = exchange(grads[:, half:])
    total = (grads[:, :half].astype(jnp.float32) + grads_other.astype(jnp.float32)).astype(
        jnp.bfloat16
    )
    back = everywhere(total)
    grad_qk = by_token(back[:, :, :HEAD_DIM])
    grad_values = by_token(back[:, :, HEAD_DIM:])

    mixed = contract(attended_rows, whole_weight, 1, 1).astype(jnp.bfloat16)

    plane = peers // PLANES
    groups = [[level * plane + place for place in range(plane)] for level in range(PLANES)]
    plane_grad = lax.all_gather(out_grad, "ctx", axis=0, tiled=True, axis_index_groups=groups)
    plane_attended = lax.all_to_all(
        attended_rows, "ctx", split_axis=1, concat_axis=0, tiled=True, axis_index_groups=groups
    )
    partial = contract(plane_grad, plane_attended, 0, 0) * (1.0 / math.sqrt(token_rows * peers))
    shares = everywhere(
        partial.astype(jnp.bfloat16).reshape(peers, row_width // peers, row_width // plane)
    )
    shares = shares.reshape((PLANES, plane) + shares.shape[1:]).astype(jnp.float32)
    grad_weight = jnp.sum(shares, axis=0).transpose(1, 0, 2).reshape(-1, row_width)
    return (mixed, grad_qk, grad_values, grad_weight)


def per_device(shared_qk, values, out_grad, out_weight, buckets):
    token_rows, row_width = shared_qk.shape
    peers = lax.axis_size("ctx")
    fits = (
        lax.axis_size("head") == 1
        and buckets.shape[0] == 2
        and peers == 2 * (row_width // HEAD_DIM)
        and 2 * token_rows == TALL
        and TALL // peers == 8
    )
    whole = head_owner_device if fits else bucket_owner_device
    return whole(shared_qk, values, out_grad, out_weight, buckets)


def solution(mesh):
    in_specs = (
        P("ctx", "head"),
        P("ctx", "head"),
        P("ctx", "head"),
        P("ctx", "head"),
        P(None, "ctx"),
    )
    out_specs = (P("ctx", "head"), P("ctx", "head"), P("ctx", "head"), P("ctx", "head"))
    return jax.shard_map(
        per_device, mesh=mesh, in_specs=in_specs, out_specs=out_specs, check_vma=False
    )
```

```python
import math

import jax
import jax.numpy as jnp
from jax import lax
from jax.experimental import pallas as pl
from jax.experimental.pallas import tpu as pltpu
from jax.sharding import PartitionSpec as P

HEAD_DIM = 128
SPAN = 128


self_penalty = 10000.0
masked_score = -1e30


def with_zero_row(matrix):
    return jnp.concatenate([matrix, jnp.zeros((1,) + matrix.shape[1:], matrix.dtype)], axis=0)


def key_windows(rows):
    row_count = rows.shape[0]
    leading = jnp.zeros((SPAN,) + rows.shape[1:], rows.dtype)
    earlier = jnp.concatenate([leading, rows[: row_count - SPAN]], axis=0)
    shape_out = (row_count // SPAN, SPAN) + rows.shape[1:]
    return jnp.concatenate([earlier.reshape(shape_out), rows.reshape(shape_out)], axis=1)


def fold_windows(stacked):
    current = stacked[:, SPAN:]
    earlier = stacked[:, :SPAN]
    return current + jnp.concatenate([earlier[1:], jnp.zeros_like(earlier[:1])], axis=0)


def span_probs(queries, key_rows, key_live):
    scores = jnp.einsum(
        "qhd,khd->hqk", queries, key_rows, preferred_element_type=jnp.float32
    ) * HEAD_DIM ** (-0.5)
    itself = jnp.arange(2 * SPAN)[None, :] == jnp.arange(SPAN)[:, None] + SPAN
    scores = jnp.where(itself[None], scores - self_penalty, scores)
    scores = jnp.where(key_live[None, None, :], scores, masked_score)
    largest = jnp.max(scores, axis=-1, keepdims=True)
    lifted = jnp.exp(scores - largest)
    summed = jnp.sum(lifted, axis=-1, keepdims=True)
    return (lifted / summed, (largest + jnp.log(summed))[..., 0])


def owner_forward(own_qk, own_values, occupied, local_heads):
    blocks = own_qk.shape[0] // SPAN
    queries = own_qk.reshape(blocks, SPAN, local_heads, HEAD_DIM)
    key_rows = key_windows(own_qk).reshape(blocks, 2 * SPAN, local_heads, HEAD_DIM)
    value_rows = key_windows(own_values).reshape(blocks, 2 * SPAN, local_heads, HEAD_DIM)
    live_keys = key_windows(occupied)

    def one_block(pieces):
        block_query, block_key, block_value, block_live = pieces
        probability, log_total = span_probs(block_query, block_key, block_live)
        result = jnp.einsum(
            "hqk,khd->qhd",
            probability.astype(jnp.bfloat16),
            block_value,
            preferred_element_type=jnp.float32,
        )
        return (result.astype(jnp.bfloat16).reshape(SPAN, local_heads * HEAD_DIM), log_total.T)

    outputs, log_totals = lax.map(one_block, (queries, key_rows, value_rows, live_keys))
    return (outputs.reshape(-1, local_heads * HEAD_DIM), log_totals.reshape(-1, local_heads))


def owner_backward(own_qk, own_values, occupied, own_grad, own_shift, local_heads):
    blocks = own_qk.shape[0] // SPAN
    queries = own_qk.reshape(blocks, SPAN, local_heads, HEAD_DIM)
    key_rows = key_windows(own_qk).reshape(blocks, 2 * SPAN, local_heads, HEAD_DIM)
    value_rows = key_windows(own_values).reshape(blocks, 2 * SPAN, local_heads, HEAD_DIM)
    live_keys = key_windows(occupied)
    grad_rows = own_grad.reshape(blocks, SPAN, local_heads, HEAD_DIM)
    shift_rows = own_shift.reshape(blocks, SPAN, local_heads)

    def one_block(pieces):
        block_query, block_key, block_value, block_live, block_grad, block_shift = pieces
        probability, log_total = span_probs(block_query, block_key, block_live)
        prob_grad = jnp.einsum(
            "qhd,khd->hqk", block_grad, block_value, preferred_element_type=jnp.float32
        )
        score_grad = (probability * (prob_grad - block_shift.T[:, :, None])).astype(jnp.bfloat16)
        query_grad = jnp.einsum(
            "hqk,khd->qhd", score_grad, block_key, preferred_element_type=jnp.float32
        ) * HEAD_DIM ** (-0.5)
        key_grad = jnp.einsum(
            "hqk,qhd->khd", score_grad, block_query, preferred_element_type=jnp.float32
        ) * HEAD_DIM ** (-0.5)
        value_grad = jnp.einsum(
            "hqk,qhd->khd",
            probability.astype(jnp.bfloat16),
            block_grad,
            preferred_element_type=jnp.float32,
        )
        return (query_grad, key_grad, value_grad)

    query_grad, key_grad, value_grad = lax.map(
        one_block, (queries, key_rows, value_rows, live_keys, grad_rows, shift_rows)
    )
    row_width = local_heads * HEAD_DIM
    qk_rows = (query_grad + fold_windows(key_grad)).reshape(-1, row_width).astype(jnp.bfloat16)
    value_out = fold_windows(value_grad).reshape(-1, row_width).astype(jnp.bfloat16)
    return (qk_rows, value_out)


def route_round(bucket_row, peer_count, per_peer, token_rows):
    owners = jnp.arange(peer_count, dtype=jnp.int32)
    member = (bucket_row[:, None] == owners[None, :]).astype(jnp.int32)
    earlier = jnp.cumsum(member, axis=0) - member
    position = jnp.sum(earlier * member, axis=1)
    slot_index = bucket_row * per_peer + position
    slot_token = (
        jnp.full((peer_count * per_peer,), token_rows, jnp.int32)
        .at[slot_index]
        .set(jnp.arange(token_rows, dtype=jnp.int32))
    )
    return (slot_index, slot_token)


def compact_slots(slot_marks, capacity):
    target = jnp.cumsum(slot_marks) - 1
    target = jnp.where(slot_marks > 0, target, capacity).astype(jnp.int32)
    source_slot = (
        jnp.full((capacity,), capacity, jnp.int32)
        .at[target]
        .set(jnp.arange(capacity, dtype=jnp.int32), mode="drop")
    )
    return (source_slot, target)


def bucket_owner_device(shared_qk, values, out_grad, out_weight, buckets):
    token_rows, row_width = shared_qk.shape
    local_heads = row_width // HEAD_DIM
    peer_count = lax.axis_size("ctx")
    capacity = 2 * token_rows
    per_peer = capacity // peer_count
    rounds = buckets.shape[0]
    routes = [
        route_round(buckets[round_index], peer_count, per_peer, token_rows)
        for round_index in range(rounds)
    ]
    padded_qk = with_zero_row(shared_qk)
    padded_values = with_zero_row(values)
    whole_weight = lax.all_gather(out_weight, "ctx", axis=0, tiled=True)
    groups = [[round_index] for round_index in range(rounds)]

    def outgoing(matrix, round_index):
        return matrix[routes[round_index][1]].reshape((peer_count, per_peer) + matrix.shape[1:])

    def homeward(received, round_index):
        flat_rows = received.reshape((peer_count * per_peer,) + received.shape[2:])
        return flat_rows[routes[round_index][0]]

    round_outputs = [None] * rounds
    round_logs = [None] * rounds
    owner_state = [None] * rounds
    for round_group in groups:
        send_qk = jnp.stack(
            [outgoing(padded_qk, round_index) for round_index in round_group], axis=1
        )
        send_values = jnp.stack(
            [outgoing(padded_values, round_index) for round_index in round_group], axis=1
        )
        slot_marks = jnp.stack(
            [
                (routes[round_index][1] < token_rows)
                .astype(jnp.int32)
                .reshape(peer_count, per_peer)
                for round_index in round_group
            ],
            axis=1,
        )
        got_qk, got_values, got_marks = (
            lax.all_to_all(send_qk, "ctx", split_axis=0, concat_axis=0, tiled=True),
            lax.all_to_all(send_values, "ctx", split_axis=0, concat_axis=0, tiled=True),
            lax.all_to_all(slot_marks, "ctx", split_axis=0, concat_axis=0, tiled=True),
        )
        returned_rows = []
        returned_logs = []
        for member_index, round_index in enumerate(round_group):
            source_slot, target = compact_slots(got_marks[:, member_index].reshape(-1), capacity)
            own_qk = with_zero_row(got_qk[:, member_index].reshape(capacity, row_width))[
                source_slot
            ]
            own_values = with_zero_row(got_values[:, member_index].reshape(capacity, row_width))[
                source_slot
            ]
            occupied = source_slot < capacity
            rows_out, logs_out = owner_forward(own_qk, own_values, occupied, local_heads)
            owner_state[round_index] = (own_qk, own_values, occupied, source_slot, target)
            returned_rows.append(
                with_zero_row(rows_out)[target].reshape(peer_count, per_peer, row_width)
            )
            returned_logs.append(
                with_zero_row(logs_out)[target].reshape(peer_count, per_peer, local_heads)
            )
        back_rows, back_logs = (
            lax.all_to_all(
                jnp.stack(returned_rows, axis=1).astype(jnp.float32),
                "ctx",
                split_axis=0,
                concat_axis=0,
                tiled=True,
            ).astype(jnp.bfloat16),
            lax.all_to_all(
                jnp.stack(returned_logs, axis=1), "ctx", split_axis=0, concat_axis=0, tiled=True
            ),
        )
        for member_index, round_index in enumerate(round_group):
            round_outputs[round_index] = homeward(back_rows[:, member_index], round_index)
            round_logs[round_index] = homeward(back_logs[:, member_index], round_index)
    log_stack = jnp.stack(round_logs)
    largest = jnp.max(log_stack, axis=0)
    lifted = jnp.exp(log_stack - largest)
    round_weight = lifted / jnp.sum(lifted, axis=0)
    row_stack = (
        jnp.stack(round_outputs)
        .astype(jnp.float32)
        .reshape(rounds, token_rows, local_heads, HEAD_DIM)
    )
    attended = (
        jnp.sum(round_weight[..., None] * row_stack, axis=0)
        .reshape(token_rows, row_width)
        .astype(jnp.bfloat16)
    )
    partial_value = lax.dot_general(
        attended, whole_weight, (((1,), (1,)), ((), ())), preferred_element_type=jnp.float32
    )
    mixed = lax.psum_scatter(partial_value, "head", scatter_dimension=1, tiled=True).astype(
        jnp.bfloat16
    )
    full_grad = lax.all_gather(out_grad, "head", axis=1, tiled=True)
    attended_grad = jnp.dot(full_grad, whole_weight, preferred_element_type=jnp.float32)
    token_total = token_rows * peer_count
    grad_weight = lax.psum_scatter(
        lax.dot_general(
            full_grad, attended, (((0,), (0,)), ((), ())), preferred_element_type=jnp.float32
        ),
        "ctx",
        scatter_dimension=0,
        tiled=True,
    ) * (1.0 / math.sqrt(token_total))
    grad_heads = attended_grad.reshape(token_rows, local_heads, HEAD_DIM)
    inner = jnp.sum(
        grad_heads * attended.astype(jnp.float32).reshape(token_rows, local_heads, HEAD_DIM),
        axis=-1,
    )
    qk_total = jnp.zeros((token_rows, row_width), jnp.float32)
    value_total = jnp.zeros((token_rows, row_width), jnp.float32)
    for round_group in groups:
        send_grad = jnp.stack(
            [
                outgoing(
                    with_zero_row(
                        (round_weight[round_index][..., None] * grad_heads)
                        .reshape(token_rows, row_width)
                        .astype(jnp.bfloat16)
                    ),
                    round_index,
                )
                for round_index in round_group
            ],
            axis=1,
        )
        send_shift = jnp.stack(
            [
                outgoing(with_zero_row(round_weight[round_index] * inner), round_index)
                for round_index in round_group
            ],
            axis=1,
        )
        got_grad, got_shift = (
            lax.all_to_all(
                send_grad.astype(jnp.float32), "ctx", split_axis=0, concat_axis=0, tiled=True
            ).astype(send_grad.dtype),
            lax.all_to_all(send_shift, "ctx", split_axis=0, concat_axis=0, tiled=True),
        )
        returned_qk = []
        returned_values = []
        for member_index, round_index in enumerate(round_group):
            own_qk, own_values, occupied, source_slot, target = owner_state[round_index]
            own_grad = with_zero_row(got_grad[:, member_index].reshape(capacity, row_width))[
                source_slot
            ]
            own_shift = with_zero_row(got_shift[:, member_index].reshape(capacity, local_heads))[
                source_slot
            ]
            qk_rows, value_rows = owner_backward(
                own_qk, own_values, occupied, own_grad, own_shift, local_heads
            )
            returned_qk.append(
                with_zero_row(qk_rows)[target].reshape(peer_count, per_peer, row_width)
            )
            returned_values.append(
                with_zero_row(value_rows)[target].reshape(peer_count, per_peer, row_width)
            )
        back_qk, back_values = (
            lax.all_to_all(
                jnp.stack(returned_qk, axis=1), "ctx", split_axis=0, concat_axis=0, tiled=True
            ),
            lax.all_to_all(
                jnp.stack(returned_values, axis=1), "ctx", split_axis=0, concat_axis=0, tiled=True
            ),
        )
        for member_index, round_index in enumerate(round_group):
            qk_total = qk_total + homeward(back_qk[:, member_index], round_index).astype(
                jnp.float32
            )
            value_total = value_total + homeward(back_values[:, member_index], round_index).astype(
                jnp.float32
            )
    return (mixed, qk_total.astype(jnp.bfloat16), value_total.astype(jnp.bfloat16), grad_weight)


PLANES = 4
TALL = 256
HALF = 64
VMEM_BYTES = 48 * 1024 * 1024


def contract(left, right, left_dim, right_dim):
    return lax.dot_general(
        left, right, (((left_dim,), (right_dim,)), ((), ())), preferred_element_type=jnp.float32
    )


def slot_pick(slot_ref, source):
    slot_ids = lax.broadcasted_iota(jnp.int32, (TALL, SPAN), 0)
    return (slot_ids == slot_ref[pl.ds(source, 1), :]).astype(jnp.bfloat16)


def bucket_scores(rows, code_ref, bucket):
    scores = contract(rows, rows, 1, 1) * HEAD_DIM ** (-0.5)
    key_ids = lax.broadcasted_iota(jnp.int32, (TALL, TALL), 0)
    query_ids = lax.broadcasted_iota(jnp.int32, (TALL, TALL), 1)
    scores = jnp.where(key_ids == query_ids, scores - self_penalty, scores)
    code_row = code_ref[pl.ds(bucket, 1), :]
    code_column = jnp.broadcast_to(code_row, (SPAN, TALL)).T
    code_column = jnp.concatenate([code_column, code_column], axis=1)
    seen = (code_column > 0.5) & (code_column <= jnp.maximum(code_row, 1.0))
    return jnp.where(seen, scores, masked_score)


def forward_kernel(mine_ref, other_ref, slot_ref, code_ref, out_ref, log_ref, grouped, results):
    sources, slots = grouped.shape[0], grouped.shape[1]
    per_peer = TALL // sources
    buckets = slots // per_peer

    def group(source, carry):
        rows = jnp.concatenate([mine_ref[source, :HALF], other_ref[source]], axis=0)
        grouped[source] = contract(slot_pick(slot_ref, source), rows, 1, 0)
        return carry

    lax.fori_loop(0, sources, group, 0, unroll=2)

    def attend(bucket, carry):
        place = pl.ds(pl.multiple_of(bucket * per_peer, per_peer), per_peer)
        rows = grouped[:, place, :].reshape(TALL, 2 * HEAD_DIM).astype(jnp.bfloat16)
        scores = bucket_scores(rows[:, :HEAD_DIM], code_ref, bucket)
        largest = jnp.max(scores, axis=0, keepdims=True)
        lifted = jnp.exp(scores - largest)
        summed = jnp.sum(lifted, axis=0, keepdims=True)
        probability = (lifted / summed).astype(jnp.bfloat16)
        result = contract(probability, rows[:, HEAD_DIM:], 0, 0)
        results[:, place, :] = result.reshape(sources, per_peer, HEAD_DIM)
        log_ref[pl.ds(bucket, 1), :] = largest + jnp.log(summed)
        return carry

    lax.fori_loop(0, buckets, attend, 0, unroll=2)

    def scatter(source, carry):
        rows = results[source].astype(jnp.bfloat16)
        out_ref[source] = contract(slot_pick(slot_ref, source), rows, 0, 0).astype(jnp.bfloat16)
        return carry

    lax.fori_loop(0, sources, scatter, 0, unroll=2)


def backward_kernel(
    mine_ref, other_ref, grad_ref, slot_ref, code_ref, log_ref, shift_ref, out_ref, grouped, results
):
    sources, slots = grouped.shape[0], grouped.shape[1]
    per_peer = TALL // sources
    buckets = slots // per_peer
    both = 2 * HEAD_DIM

    def group(source, carry):
        rows = jnp.concatenate([mine_ref[source, :HALF], other_ref[source]], axis=0)
        pick = slot_pick(slot_ref, source)
        grouped[source, :, :both] = contract(pick, rows, 1, 0)
        grouped[source, :, both:] = contract(pick, grad_ref[source], 1, 0)
        return carry

    lax.fori_loop(0, sources, group, 0, unroll=2)

    def attend(bucket, carry):
        place = pl.ds(pl.multiple_of(bucket * per_peer, per_peer), per_peer)
        rows = grouped[:, place, :].reshape(TALL, 3 * HEAD_DIM).astype(jnp.bfloat16)
        qk_rows, value_rows, grad_rows = (
            rows[:, :HEAD_DIM],
            rows[:, HEAD_DIM:both],
            rows[:, both:],
        )
        scores = bucket_scores(qk_rows, code_ref, bucket)
        probability = jnp.exp(scores - log_ref[pl.ds(bucket, 1), :])
        prob_grad = contract(value_rows, grad_rows, 1, 1)
        score_grad = (probability * (prob_grad - shift_ref[pl.ds(bucket, 1), :])).astype(
            jnp.bfloat16
        )
        qk_grad = contract(score_grad, qk_rows, 0, 0) + contract(score_grad, qk_rows, 1, 0)
        value_grad = contract(probability.astype(jnp.bfloat16), grad_rows, 1, 0)
        results[:, place, :HEAD_DIM] = (qk_grad * HEAD_DIM ** (-0.5)).reshape(
            sources, per_peer, HEAD_DIM
        )
        results[:, place, HEAD_DIM:] = value_grad.reshape(sources, per_peer, HEAD_DIM)
        return carry

    lax.fori_loop(0, buckets, attend, 0, unroll=2)

    def scatter(source, carry):
        rows = results[source].astype(jnp.bfloat16)
        out_ref[source] = contract(slot_pick(slot_ref, source), rows, 0, 0).astype(jnp.bfloat16)
        return carry

    lax.fori_loop(0, sources, scatter, 0, unroll=2)


def kernel_call(body, out_shape, scratch_shapes, arguments):
    return pl.pallas_call(
        body,
        out_shape=out_shape,
        in_specs=[pl.BlockSpec(memory_space=pltpu.VMEM)] * len(arguments),
        out_specs=jax.tree.map(lambda _: pl.BlockSpec(memory_space=pltpu.VMEM), out_shape),
        scratch_shapes=scratch_shapes,
        compiler_params=pltpu.CompilerParams(vmem_limit_bytes=VMEM_BYTES),
    )(*arguments)


def head_owner_device(shared_qk, values, out_grad, out_weight, buckets):
    token_rows, row_width = shared_qk.shape
    heads = row_width // HEAD_DIM
    peers = lax.axis_size("ctx")
    per_peer = 2 * token_rows // peers
    half = token_rows // 2
    slots = peers * per_peer
    core = lax.axis_index("ctx") % 2
    first = core == 0
    partners = [(device, device ^ 1) for device in range(peers)]

    def exchange(block):
        return lax.ppermute(block, "ctx", partners)

    def swapped(block):
        return jnp.concatenate([block[:, half:], block[:, :half]], axis=1)

    def everywhere(block):
        return lax.all_to_all(block, "ctx", split_axis=0, concat_axis=0, tiled=True)

    def by_head(rows):
        return rows.reshape(2, half, heads, HEAD_DIM).transpose(2, 0, 1, 3)

    def by_token(blocks):
        return blocks.reshape(heads, 2, half, HEAD_DIM).transpose(1, 2, 0, 3).reshape(
            token_rows, row_width
        )

    def own_half(rows):
        parted = rows.reshape(rows.shape[0], heads, 2, -1)
        even, odd = parted[:, :, 0], parted[:, :, 1]
        kept, passed = jnp.where(first, even, odd), jnp.where(first, odd, even)
        return kept.reshape(rows.shape[0], -1), passed.reshape(rows.shape[0], -1)

    def moved(block, mask):
        return lax.ppermute(block, "ctx", [(device, device ^ mask) for device in range(peers)])

    half_weight = lax.all_gather(
        out_weight,
        "ctx",
        axis=0,
        tiled=True,
        axis_index_groups=[list(range(0, peers, 2)), list(range(1, peers, 2))],
    )

    tag = jnp.pad(buckets.astype(jnp.bfloat16).reshape(1, -1), ((0, 7), (0, 0)))
    sent = jnp.concatenate([by_head(shared_qk), by_head(values)], axis=-1)
    sent = jnp.concatenate(
        [
            sent.reshape(peers, half, 2 * HEAD_DIM),
            jnp.broadcast_to(tag[None], (peers, 8, 2 * HEAD_DIM)),
        ],
        axis=1,
    )
    mine = everywhere(sent)
    other = exchange(mine[:, :half])

    all_buckets = mine[:, half].astype(jnp.int32).reshape(peers, 2, token_rows)
    own = jnp.where(first, all_buckets[:, 0], all_buckets[:, 1])
    order = jnp.arange(token_rows, dtype=jnp.int32)
    same = (own[:, :, None] == own[:, None, :]) & (order[None, :] < order[:, None])[None]
    position = jnp.sum(same.astype(jnp.int32), axis=2)
    slot = own * per_peer + position
    slot = jnp.where(first, slot, swapped(slot))
    bucket_ids = jnp.arange(peers, dtype=jnp.int32)
    counts = jnp.sum((own[:, :, None] == bucket_ids).astype(jnp.int32), axis=1)
    before = (bucket_ids[None, :] < bucket_ids[:, None]).astype(jnp.int32)
    starts = jnp.sum(before[:, :, None] * counts[None], axis=1)
    within = jnp.arange(per_peer, dtype=jnp.int32)
    live = within < counts[:, :, None]
    code = jnp.where(live, jnp.where(starts[:, :, None] + within >= SPAN, 2.0, 1.0), 0.0)
    code = code.astype(jnp.float32).transpose(1, 0, 2).reshape(peers, peers * per_peer)

    result, log_slots = kernel_call(
        forward_kernel,
        (
            jax.ShapeDtypeStruct((peers, token_rows, HEAD_DIM), jnp.bfloat16),
            jax.ShapeDtypeStruct((peers, peers * per_peer), jnp.float32),
        ),
        [
            pltpu.VMEM((peers, slots, 2 * HEAD_DIM), jnp.float32),
            pltpu.VMEM((peers, slots, HEAD_DIM), jnp.float32),
        ],
        (mine, other, slot, code),
    )

    grad_kept, grad_passed = own_half(out_grad)
    grad_pair = jnp.concatenate([grad_kept, exchange(grad_passed)], axis=0)
    grad_part = jnp.dot(grad_pair, half_weight, preferred_element_type=jnp.float32)
    attended_grad = (grad_part[:token_rows] + exchange(grad_part[token_rows:])).astype(
        jnp.bfloat16
    )
    grad_mine = everywhere(by_head(attended_grad).reshape(peers, half, HEAD_DIM))
    grad_rows = jnp.concatenate([grad_mine, exchange(grad_mine)], axis=1).astype(jnp.float32)

    chosen = slot[:, :, None] == jnp.arange(slots, dtype=jnp.int32)
    log_by_source = log_slots.reshape(peers, peers, per_peer).transpose(1, 0, 2).reshape(peers, slots)
    log_own = jnp.sum(jnp.where(chosen, log_by_source[:, None, :], 0.0), axis=2)
    log_other = swapped(exchange(log_own))
    result_other = swapped(exchange(result))
    largest = jnp.maximum(log_own, log_other)
    lifted_own, lifted_other = jnp.exp(log_own - largest), jnp.exp(log_other - largest)
    lifted_sum = lifted_own + lifted_other
    weight_own, weight_other = lifted_own / lifted_sum, lifted_other / lifted_sum
    attended = (
        weight_own[:, :, None] * result.astype(jnp.float32)
        + weight_other[:, :, None] * result_other.astype(jnp.float32)
    ).astype(jnp.bfloat16)

    inner = jnp.sum(grad_rows * attended.astype(jnp.float32), axis=-1)
    shift = weight_own * inner
    query_grad = (weight_own[:, :, None] * grad_rows).astype(jnp.bfloat16)
    shift_slots = jnp.sum(jnp.where(chosen, shift[:, :, None], 0.0), axis=1)
    shift_slots = (
        shift_slots.reshape(peers, peers, per_peer).transpose(1, 0, 2).reshape(peers, slots)
    )

    attended_rows = by_token(everywhere(attended[:, :half]))

    attended_pair = jnp.concatenate([attended_rows, exchange(attended_rows)], axis=0)
    mixed_part = contract(attended_pair, half_weight, 1, 1).astype(jnp.bfloat16)
    mixed_kept, mixed_got = mixed_part[:token_rows], exchange(mixed_part[token_rows:])
    mixed_even = jnp.where(first, mixed_kept, mixed_got).reshape(token_rows, heads, 1, -1)
    mixed_odd = jnp.where(first, mixed_got, mixed_kept).reshape(token_rows, heads, 1, -1)
    mixed = jnp.concatenate([mixed_even, mixed_odd], axis=2).reshape(token_rows, row_width)

    plane = peers // PLANES
    groups = [[level * plane + place for place in range(plane)] for level in range(PLANES)]
    plane_attended = lax.all_to_all(
        attended_rows, "ctx", split_axis=1, concat_axis=0, tiled=True, axis_index_groups=groups
    ).reshape(plane, token_rows, row_width // plane)
    here = lax.axis_index("ctx") % plane
    plane_attended = jnp.concatenate(
        [
            lax.dynamic_index_in_dim(plane_attended, here ^ mask, axis=0, keepdims=False)
            for mask in (0, 2, 4, 6, 1, 3, 5, 7)
        ],
        axis=0,
    )
    left, right = out_grad[:, : row_width // 2], out_grad[:, row_width // 2 :]
    left_two = jnp.concatenate([left, moved(left, 2)], axis=0)
    right_x = moved(right, 4)
    right_two = jnp.concatenate([right, right_x], axis=0)
    left_four = jnp.concatenate([left_two, moved(left_two, 4)], axis=0)
    right_far = moved(right_two, 2)
    right_four = jnp.concatenate(
        [right, right_far[:token_rows], right_x, right_far[token_rows:]], axis=0
    )
    core_grad = jnp.concatenate([left_four, right_four], axis=1)
    plane_grad = jnp.concatenate([core_grad, exchange(core_grad)], axis=0)
    partial = contract(plane_grad, plane_attended, 0, 0) * (1.0 / math.sqrt(token_rows * peers))
    partial = partial.astype(jnp.bfloat16).reshape(
        peers, row_width // peers, row_width // plane
    )
    query_grad, partial = lax.optimization_barrier((query_grad, partial))
    shares = everywhere(partial)
    shares = shares.reshape((PLANES, plane) + shares.shape[1:]).astype(jnp.float32)
    grad_weight = jnp.sum(shares, axis=0).transpose(1, 0, 2).reshape(-1, row_width)

    grads = kernel_call(
        backward_kernel,
        jax.ShapeDtypeStruct((peers, token_rows, 2 * HEAD_DIM), jnp.bfloat16),
        [
            pltpu.VMEM((peers, slots, 3 * HEAD_DIM), jnp.float32),
            pltpu.VMEM((peers, slots, 2 * HEAD_DIM), jnp.float32),
        ],
        (mine, other, query_grad, slot, code, log_slots, shift_slots),
    )
    grads_other = exchange(grads[:, half:])
    total = (grads[:, :half].astype(jnp.float32) + grads_other.astype(jnp.float32)).astype(
        jnp.bfloat16
    )
    back = everywhere(total)
    grad_qk = by_token(back[:, :, :HEAD_DIM])
    grad_values = by_token(back[:, :, HEAD_DIM:])

    return (mixed, grad_qk, grad_values, grad_weight)


def per_device(shared_qk, values, out_grad, out_weight, buckets):
    token_rows, row_width = shared_qk.shape
    peers = lax.axis_size("ctx")
    fits = (
        lax.axis_size("head") == 1
        and buckets.shape[0] == 2
        and peers == 2 * (row_width // HEAD_DIM)
        and 2 * token_rows == TALL
        and TALL // peers == 8
    )
    whole = head_owner_device if fits else bucket_owner_device
    return whole(shared_qk, values, out_grad, out_weight, buckets)


def solution(mesh):
    in_specs = (
        P("ctx", "head"),
        P("ctx", "head"),
        P("ctx", "head"),
        P("ctx", "head"),
        P(None, "ctx"),
    )
    out_specs = (P("ctx", "head"), P("ctx", "head"), P("ctx", "head"), P("ctx", "head"))
    return jax.shard_map(
        per_device, mesh=mesh, in_specs=in_specs, out_specs=out_specs, check_vma=False
    )
```

```python
import math

import jax
import jax.numpy as jnp
from jax import lax
from jax.experimental import pallas as pl
from jax.experimental.pallas import tpu as pltpu
from jax.sharding import PartitionSpec as P

HEAD_DIM = 128
SPAN = 128


self_penalty = 10000.0
masked_score = -1e30


def with_zero_row(matrix):
    return jnp.concatenate([matrix, jnp.zeros((1,) + matrix.shape[1:], matrix.dtype)], axis=0)


def key_windows(rows):
    row_count = rows.shape[0]
    leading = jnp.zeros((SPAN,) + rows.shape[1:], rows.dtype)
    earlier = jnp.concatenate([leading, rows[: row_count - SPAN]], axis=0)
    shape_out = (row_count // SPAN, SPAN) + rows.shape[1:]
    return jnp.concatenate([earlier.reshape(shape_out), rows.reshape(shape_out)], axis=1)


def fold_windows(stacked):
    current = stacked[:, SPAN:]
    earlier = stacked[:, :SPAN]
    return current + jnp.concatenate([earlier[1:], jnp.zeros_like(earlier[:1])], axis=0)


def span_probs(queries, key_rows, key_live):
    scores = jnp.einsum(
        "qhd,khd->hqk", queries, key_rows, preferred_element_type=jnp.float32
    ) * HEAD_DIM ** (-0.5)
    itself = jnp.arange(2 * SPAN)[None, :] == jnp.arange(SPAN)[:, None] + SPAN
    scores = jnp.where(itself[None], scores - self_penalty, scores)
    scores = jnp.where(key_live[None, None, :], scores, masked_score)
    largest = jnp.max(scores, axis=-1, keepdims=True)
    lifted = jnp.exp(scores - largest)
    summed = jnp.sum(lifted, axis=-1, keepdims=True)
    return (lifted / summed, (largest + jnp.log(summed))[..., 0])


def owner_forward(own_qk, own_values, occupied, local_heads):
    blocks = own_qk.shape[0] // SPAN
    queries = own_qk.reshape(blocks, SPAN, local_heads, HEAD_DIM)
    key_rows = key_windows(own_qk).reshape(blocks, 2 * SPAN, local_heads, HEAD_DIM)
    value_rows = key_windows(own_values).reshape(blocks, 2 * SPAN, local_heads, HEAD_DIM)
    live_keys = key_windows(occupied)

    def one_block(pieces):
        block_query, block_key, block_value, block_live = pieces
        probability, log_total = span_probs(block_query, block_key, block_live)
        result = jnp.einsum(
            "hqk,khd->qhd",
            probability.astype(jnp.bfloat16),
            block_value,
            preferred_element_type=jnp.float32,
        )
        return (result.astype(jnp.bfloat16).reshape(SPAN, local_heads * HEAD_DIM), log_total.T)

    outputs, log_totals = lax.map(one_block, (queries, key_rows, value_rows, live_keys))
    return (outputs.reshape(-1, local_heads * HEAD_DIM), log_totals.reshape(-1, local_heads))


def owner_backward(own_qk, own_values, occupied, own_grad, own_shift, local_heads):
    blocks = own_qk.shape[0] // SPAN
    queries = own_qk.reshape(blocks, SPAN, local_heads, HEAD_DIM)
    key_rows = key_windows(own_qk).reshape(blocks, 2 * SPAN, local_heads, HEAD_DIM)
    value_rows = key_windows(own_values).reshape(blocks, 2 * SPAN, local_heads, HEAD_DIM)
    live_keys = key_windows(occupied)
    grad_rows = own_grad.reshape(blocks, SPAN, local_heads, HEAD_DIM)
    shift_rows = own_shift.reshape(blocks, SPAN, local_heads)

    def one_block(pieces):
        block_query, block_key, block_value, block_live, block_grad, block_shift = pieces
        probability, log_total = span_probs(block_query, block_key, block_live)
        prob_grad = jnp.einsum(
            "qhd,khd->hqk", block_grad, block_value, preferred_element_type=jnp.float32
        )
        score_grad = (probability * (prob_grad - block_shift.T[:, :, None])).astype(jnp.bfloat16)
        query_grad = jnp.einsum(
            "hqk,khd->qhd", score_grad, block_key, preferred_element_type=jnp.float32
        ) * HEAD_DIM ** (-0.5)
        key_grad = jnp.einsum(
            "hqk,qhd->khd", score_grad, block_query, preferred_element_type=jnp.float32
        ) * HEAD_DIM ** (-0.5)
        value_grad = jnp.einsum(
            "hqk,qhd->khd",
            probability.astype(jnp.bfloat16),
            block_grad,
            preferred_element_type=jnp.float32,
        )
        return (query_grad, key_grad, value_grad)

    query_grad, key_grad, value_grad = lax.map(
        one_block, (queries, key_rows, value_rows, live_keys, grad_rows, shift_rows)
    )
    row_width = local_heads * HEAD_DIM
    qk_rows = (query_grad + fold_windows(key_grad)).reshape(-1, row_width).astype(jnp.bfloat16)
    value_out = fold_windows(value_grad).reshape(-1, row_width).astype(jnp.bfloat16)
    return (qk_rows, value_out)


def route_round(bucket_row, peer_count, per_peer, token_rows):
    owners = jnp.arange(peer_count, dtype=jnp.int32)
    member = (bucket_row[:, None] == owners[None, :]).astype(jnp.int32)
    earlier = jnp.cumsum(member, axis=0) - member
    position = jnp.sum(earlier * member, axis=1)
    slot_index = bucket_row * per_peer + position
    slot_token = (
        jnp.full((peer_count * per_peer,), token_rows, jnp.int32)
        .at[slot_index]
        .set(jnp.arange(token_rows, dtype=jnp.int32))
    )
    return (slot_index, slot_token)


def compact_slots(slot_marks, capacity):
    target = jnp.cumsum(slot_marks) - 1
    target = jnp.where(slot_marks > 0, target, capacity).astype(jnp.int32)
    source_slot = (
        jnp.full((capacity,), capacity, jnp.int32)
        .at[target]
        .set(jnp.arange(capacity, dtype=jnp.int32), mode="drop")
    )
    return (source_slot, target)


def bucket_owner_device(shared_qk, values, out_grad, out_weight, buckets):
    token_rows, row_width = shared_qk.shape
    local_heads = row_width // HEAD_DIM
    peer_count = lax.axis_size("ctx")
    capacity = 2 * token_rows
    per_peer = capacity // peer_count
    rounds = buckets.shape[0]
    routes = [
        route_round(buckets[round_index], peer_count, per_peer, token_rows)
        for round_index in range(rounds)
    ]
    padded_qk = with_zero_row(shared_qk)
    padded_values = with_zero_row(values)
    whole_weight = lax.all_gather(out_weight, "ctx", axis=0, tiled=True)
    groups = [[round_index] for round_index in range(rounds)]

    def outgoing(matrix, round_index):
        return matrix[routes[round_index][1]].reshape((peer_count, per_peer) + matrix.shape[1:])

    def homeward(received, round_index):
        flat_rows = received.reshape((peer_count * per_peer,) + received.shape[2:])
        return flat_rows[routes[round_index][0]]

    round_outputs = [None] * rounds
    round_logs = [None] * rounds
    owner_state = [None] * rounds
    for round_group in groups:
        send_qk = jnp.stack(
            [outgoing(padded_qk, round_index) for round_index in round_group], axis=1
        )
        send_values = jnp.stack(
            [outgoing(padded_values, round_index) for round_index in round_group], axis=1
        )
        slot_marks = jnp.stack(
            [
                (routes[round_index][1] < token_rows)
                .astype(jnp.int32)
                .reshape(peer_count, per_peer)
                for round_index in round_group
            ],
            axis=1,
        )
        got_qk, got_values, got_marks = (
            lax.all_to_all(send_qk, "ctx", split_axis=0, concat_axis=0, tiled=True),
            lax.all_to_all(send_values, "ctx", split_axis=0, concat_axis=0, tiled=True),
            lax.all_to_all(slot_marks, "ctx", split_axis=0, concat_axis=0, tiled=True),
        )
        returned_rows = []
        returned_logs = []
        for member_index, round_index in enumerate(round_group):
            source_slot, target = compact_slots(got_marks[:, member_index].reshape(-1), capacity)
            own_qk = with_zero_row(got_qk[:, member_index].reshape(capacity, row_width))[
                source_slot
            ]
            own_values = with_zero_row(got_values[:, member_index].reshape(capacity, row_width))[
                source_slot
            ]
            occupied = source_slot < capacity
            rows_out, logs_out = owner_forward(own_qk, own_values, occupied, local_heads)
            owner_state[round_index] = (own_qk, own_values, occupied, source_slot, target)
            returned_rows.append(
                with_zero_row(rows_out)[target].reshape(peer_count, per_peer, row_width)
            )
            returned_logs.append(
                with_zero_row(logs_out)[target].reshape(peer_count, per_peer, local_heads)
            )
        back_rows, back_logs = (
            lax.all_to_all(
                jnp.stack(returned_rows, axis=1).astype(jnp.float32),
                "ctx",
                split_axis=0,
                concat_axis=0,
                tiled=True,
            ).astype(jnp.bfloat16),
            lax.all_to_all(
                jnp.stack(returned_logs, axis=1), "ctx", split_axis=0, concat_axis=0, tiled=True
            ),
        )
        for member_index, round_index in enumerate(round_group):
            round_outputs[round_index] = homeward(back_rows[:, member_index], round_index)
            round_logs[round_index] = homeward(back_logs[:, member_index], round_index)
    log_stack = jnp.stack(round_logs)
    largest = jnp.max(log_stack, axis=0)
    lifted = jnp.exp(log_stack - largest)
    round_weight = lifted / jnp.sum(lifted, axis=0)
    row_stack = (
        jnp.stack(round_outputs)
        .astype(jnp.float32)
        .reshape(rounds, token_rows, local_heads, HEAD_DIM)
    )
    attended = (
        jnp.sum(round_weight[..., None] * row_stack, axis=0)
        .reshape(token_rows, row_width)
        .astype(jnp.bfloat16)
    )
    partial_value = lax.dot_general(
        attended, whole_weight, (((1,), (1,)), ((), ())), preferred_element_type=jnp.float32
    )
    mixed = lax.psum_scatter(partial_value, "head", scatter_dimension=1, tiled=True).astype(
        jnp.bfloat16
    )
    full_grad = lax.all_gather(out_grad, "head", axis=1, tiled=True)
    attended_grad = jnp.dot(full_grad, whole_weight, preferred_element_type=jnp.float32)
    token_total = token_rows * peer_count
    grad_weight = lax.psum_scatter(
        lax.dot_general(
            full_grad, attended, (((0,), (0,)), ((), ())), preferred_element_type=jnp.float32
        ),
        "ctx",
        scatter_dimension=0,
        tiled=True,
    ) * (1.0 / math.sqrt(token_total))
    grad_heads = attended_grad.reshape(token_rows, local_heads, HEAD_DIM)
    inner = jnp.sum(
        grad_heads * attended.astype(jnp.float32).reshape(token_rows, local_heads, HEAD_DIM),
        axis=-1,
    )
    qk_total = jnp.zeros((token_rows, row_width), jnp.float32)
    value_total = jnp.zeros((token_rows, row_width), jnp.float32)
    for round_group in groups:
        send_grad = jnp.stack(
            [
                outgoing(
                    with_zero_row(
                        (round_weight[round_index][..., None] * grad_heads)
                        .reshape(token_rows, row_width)
                        .astype(jnp.bfloat16)
                    ),
                    round_index,
                )
                for round_index in round_group
            ],
            axis=1,
        )
        send_shift = jnp.stack(
            [
                outgoing(with_zero_row(round_weight[round_index] * inner), round_index)
                for round_index in round_group
            ],
            axis=1,
        )
        got_grad, got_shift = (
            lax.all_to_all(
                send_grad.astype(jnp.float32), "ctx", split_axis=0, concat_axis=0, tiled=True
            ).astype(send_grad.dtype),
            lax.all_to_all(send_shift, "ctx", split_axis=0, concat_axis=0, tiled=True),
        )
        returned_qk = []
        returned_values = []
        for member_index, round_index in enumerate(round_group):
            own_qk, own_values, occupied, source_slot, target = owner_state[round_index]
            own_grad = with_zero_row(got_grad[:, member_index].reshape(capacity, row_width))[
                source_slot
            ]
            own_shift = with_zero_row(got_shift[:, member_index].reshape(capacity, local_heads))[
                source_slot
            ]
            qk_rows, value_rows = owner_backward(
                own_qk, own_values, occupied, own_grad, own_shift, local_heads
            )
            returned_qk.append(
                with_zero_row(qk_rows)[target].reshape(peer_count, per_peer, row_width)
            )
            returned_values.append(
                with_zero_row(value_rows)[target].reshape(peer_count, per_peer, row_width)
            )
        back_qk, back_values = (
            lax.all_to_all(
                jnp.stack(returned_qk, axis=1), "ctx", split_axis=0, concat_axis=0, tiled=True
            ),
            lax.all_to_all(
                jnp.stack(returned_values, axis=1), "ctx", split_axis=0, concat_axis=0, tiled=True
            ),
        )
        for member_index, round_index in enumerate(round_group):
            qk_total = qk_total + homeward(back_qk[:, member_index], round_index).astype(
                jnp.float32
            )
            value_total = value_total + homeward(back_values[:, member_index], round_index).astype(
                jnp.float32
            )
    return (mixed, qk_total.astype(jnp.bfloat16), value_total.astype(jnp.bfloat16), grad_weight)


PLANES = 4
TALL = 256
HALF = 64
VMEM_BYTES = 48 * 1024 * 1024


def contract(left, right, left_dim, right_dim):
    return lax.dot_general(
        left, right, (((left_dim,), (right_dim,)), ((), ())), preferred_element_type=jnp.float32
    )


def slot_pick(slot_ref, source):
    slot_ids = lax.broadcasted_iota(jnp.int32, (TALL, SPAN), 0)
    return (slot_ids == slot_ref[pl.ds(source, 1), :]).astype(jnp.bfloat16)


def bucket_scores(rows, code_ref, bucket):
    scores = contract(rows, rows, 1, 1) * HEAD_DIM ** (-0.5)
    key_ids = lax.broadcasted_iota(jnp.int32, (TALL, TALL), 0)
    query_ids = lax.broadcasted_iota(jnp.int32, (TALL, TALL), 1)
    scores = jnp.where(key_ids == query_ids, scores - self_penalty, scores)
    code_row = code_ref[pl.ds(bucket, 1), :]
    code_column = jnp.broadcast_to(code_row, (SPAN, TALL)).T
    code_column = jnp.concatenate([code_column, code_column], axis=1)
    seen = (code_column > 0.5) & (code_column <= jnp.maximum(code_row, 1.0))
    return jnp.where(seen, scores, masked_score)


def forward_kernel(mine_ref, other_ref, slot_ref, code_ref, out_ref, log_ref, grouped, results):
    sources, slots = grouped.shape[0], grouped.shape[1]
    per_peer = TALL // sources
    buckets = slots // per_peer

    def group(source, carry):
        rows = jnp.concatenate([mine_ref[source, :HALF], other_ref[source]], axis=0)
        grouped[source] = contract(slot_pick(slot_ref, source), rows, 1, 0)
        return carry

    lax.fori_loop(0, sources, group, 0, unroll=2)

    def attend(bucket, carry):
        place = pl.ds(pl.multiple_of(bucket * per_peer, per_peer), per_peer)
        rows = grouped[:, place, :].reshape(TALL, 2 * HEAD_DIM).astype(jnp.bfloat16)
        scores = bucket_scores(rows[:, :HEAD_DIM], code_ref, bucket)
        largest = jnp.max(scores, axis=0, keepdims=True)
        lifted = jnp.exp(scores - largest)
        summed = jnp.sum(lifted, axis=0, keepdims=True)
        probability = (lifted / summed).astype(jnp.bfloat16)
        result = contract(probability, rows[:, HEAD_DIM:], 0, 0)
        results[:, place, :] = result.reshape(sources, per_peer, HEAD_DIM)
        log_ref[pl.ds(bucket, 1), :] = largest + jnp.log(summed)
        return carry

    lax.fori_loop(0, buckets, attend, 0, unroll=2)

    def scatter(source, carry):
        rows = results[source].astype(jnp.bfloat16)
        out_ref[source] = contract(slot_pick(slot_ref, source), rows, 0, 0).astype(jnp.bfloat16)
        return carry

    lax.fori_loop(0, sources, scatter, 0, unroll=2)


def backward_kernel(
    mine_ref, other_ref, grad_ref, slot_ref, code_ref, log_ref, shift_ref, out_ref, grouped, results
):
    sources, slots = grouped.shape[0], grouped.shape[1]
    per_peer = TALL // sources
    buckets = slots // per_peer
    both = 2 * HEAD_DIM

    def group(source, carry):
        rows = jnp.concatenate([mine_ref[source, :HALF], other_ref[source]], axis=0)
        pick = slot_pick(slot_ref, source)
        grouped[source, :, :both] = contract(pick, rows, 1, 0)
        grouped[source, :, both:] = contract(pick, grad_ref[source], 1, 0)
        return carry

    lax.fori_loop(0, sources, group, 0, unroll=2)

    def attend(bucket, carry):
        place = pl.ds(pl.multiple_of(bucket * per_peer, per_peer), per_peer)
        rows = grouped[:, place, :].reshape(TALL, 3 * HEAD_DIM).astype(jnp.bfloat16)
        qk_rows, value_rows, grad_rows = (
            rows[:, :HEAD_DIM],
            rows[:, HEAD_DIM:both],
            rows[:, both:],
        )
        scores = bucket_scores(qk_rows, code_ref, bucket)
        probability = jnp.exp(scores - log_ref[pl.ds(bucket, 1), :])
        prob_grad = contract(value_rows, grad_rows, 1, 1)
        score_grad = (probability * (prob_grad - shift_ref[pl.ds(bucket, 1), :])).astype(
            jnp.bfloat16
        )
        qk_grad = contract(score_grad, qk_rows, 0, 0) + contract(score_grad, qk_rows, 1, 0)
        value_grad = contract(probability.astype(jnp.bfloat16), grad_rows, 1, 0)
        results[:, place, :HEAD_DIM] = (qk_grad * HEAD_DIM ** (-0.5)).reshape(
            sources, per_peer, HEAD_DIM
        )
        results[:, place, HEAD_DIM:] = value_grad.reshape(sources, per_peer, HEAD_DIM)
        return carry

    lax.fori_loop(0, buckets, attend, 0, unroll=2)

    def scatter(source, carry):
        rows = results[source].astype(jnp.bfloat16)
        out_ref[source] = contract(slot_pick(slot_ref, source), rows, 0, 0).astype(jnp.bfloat16)
        return carry

    lax.fori_loop(0, sources, scatter, 0, unroll=2)


def kernel_call(body, out_shape, scratch_shapes, arguments):
    return pl.pallas_call(
        body,
        out_shape=out_shape,
        in_specs=[pl.BlockSpec(memory_space=pltpu.VMEM)] * len(arguments),
        out_specs=jax.tree.map(lambda _: pl.BlockSpec(memory_space=pltpu.VMEM), out_shape),
        scratch_shapes=scratch_shapes,
        compiler_params=pltpu.CompilerParams(vmem_limit_bytes=VMEM_BYTES),
        cost_estimate=pl.CostEstimate(
            flops=20_000_000_000, bytes_accessed=8_000_000, transcendentals=2_000_000
        ),
    )(*arguments)


def head_owner_device(shared_qk, values, out_grad, out_weight, buckets):
    token_rows, row_width = shared_qk.shape
    heads = row_width // HEAD_DIM
    peers = lax.axis_size("ctx")
    per_peer = 2 * token_rows // peers
    half = token_rows // 2
    slots = peers * per_peer
    core = lax.axis_index("ctx") % 2
    first = core == 0
    partners = [(device, device ^ 1) for device in range(peers)]

    def exchange(block):
        return lax.ppermute(block, "ctx", partners)

    def swapped(block):
        return jnp.concatenate([block[:, half:], block[:, :half]], axis=1)

    def everywhere(block):
        return lax.all_to_all(block, "ctx", split_axis=0, concat_axis=0, tiled=True)

    def by_head(rows):
        return rows.reshape(2, half, heads, HEAD_DIM).transpose(2, 0, 1, 3)

    def by_token(blocks):
        return blocks.reshape(heads, 2, half, HEAD_DIM).transpose(1, 2, 0, 3).reshape(
            token_rows, row_width
        )

    def moved(block, mask):
        return lax.ppermute(block, "ctx", [(device, device ^ mask) for device in range(peers)])

    tag = jnp.pad(buckets.astype(jnp.bfloat16).reshape(1, -1), ((0, 7), (0, 0)))
    sent = jnp.concatenate([by_head(shared_qk), by_head(values)], axis=-1)
    sent = jnp.concatenate(
        [
            sent.reshape(peers, half, 2 * HEAD_DIM),
            jnp.broadcast_to(tag[None], (peers, 8, 2 * HEAD_DIM)),
        ],
        axis=1,
    )
    mine = everywhere(sent)
    mine, late_weight = lax.optimization_barrier((mine, out_weight))
    half_weight = lax.all_gather(
        late_weight,
        "ctx",
        axis=0,
        tiled=True,
        axis_index_groups=[list(range(0, peers, 2)), list(range(1, peers, 2))],
    )
    other = exchange(mine[:, :half])

    plane = peers // PLANES
    index = lax.axis_index("ctx")
    level, here, seat = index // plane, index % plane, index % PLANES
    masks = (0, 2, 4, 6, 1, 3, 5, 7)
    down = [
        [
            (tier * plane + place, PLANES * place + (tier - step) % PLANES)
            for tier in range(PLANES)
            for place in range(plane)
        ]
        for step in range(PLANES)
    ]

    def pick(blocks, which):
        return lax.dynamic_index_in_dim(blocks, which, axis=0, keepdims=False)

    columns = jnp.broadcast_to(
        late_weight.reshape(1, -1, plane, row_width // plane).transpose(0, 2, 1, 3),
        (PLANES, plane, row_width // peers, row_width // plane),
    ).reshape(peers, row_width // peers, row_width // plane)
    column_weight = everywhere(columns).reshape(row_width, row_width // plane)

    left, right = out_grad[:, : row_width // 2], out_grad[:, row_width // 2 :]
    left_two = jnp.concatenate([left, moved(left, 2)], axis=0)
    right_y = moved(right, 4)
    right_two = jnp.concatenate([right, right_y], axis=0)
    left_four = jnp.concatenate([left_two, moved(left_two, 4)], axis=0)
    right_far = moved(right_two, 2)
    right_four = jnp.concatenate(
        [right, right_far[:token_rows], right_y, right_far[token_rows:]], axis=0
    )
    core_grad = jnp.concatenate([left_four, right_four], axis=1)
    plane_grad = jnp.concatenate([core_grad, exchange(core_grad)], axis=0)

    all_buckets = mine[:, half].astype(jnp.int32).reshape(peers, 2, token_rows)
    own = jnp.where(first, all_buckets[:, 0], all_buckets[:, 1])
    order = jnp.arange(token_rows, dtype=jnp.int32)
    same = (own[:, :, None] == own[:, None, :]) & (order[None, :] < order[:, None])[None]
    position = jnp.sum(same.astype(jnp.int32), axis=2)
    slot = own * per_peer + position
    slot = jnp.where(first, slot, swapped(slot))
    bucket_ids = jnp.arange(peers, dtype=jnp.int32)
    counts = jnp.sum((own[:, :, None] == bucket_ids).astype(jnp.int32), axis=1)
    before = (bucket_ids[None, :] < bucket_ids[:, None]).astype(jnp.int32)
    starts = jnp.sum(before[:, :, None] * counts[None], axis=1)
    within = jnp.arange(per_peer, dtype=jnp.int32)
    live = within < counts[:, :, None]
    code = jnp.where(live, jnp.where(starts[:, :, None] + within >= SPAN, 2.0, 1.0), 0.0)
    code = code.astype(jnp.float32).transpose(1, 0, 2).reshape(peers, peers * per_peer)

    result, log_slots = kernel_call(
        forward_kernel,
        (
            jax.ShapeDtypeStruct((peers, token_rows, HEAD_DIM), jnp.bfloat16),
            jax.ShapeDtypeStruct((peers, peers * per_peer), jnp.float32),
        ),
        [
            pltpu.VMEM((peers, slots, 2 * HEAD_DIM), jnp.float32),
            pltpu.VMEM((peers, slots, HEAD_DIM), jnp.float32),
        ],
        (mine, other, slot, code),
    )

    attended_grad = (
        jnp.dot(plane_grad, column_weight, preferred_element_type=jnp.float32)
        .astype(jnp.bfloat16)
        .reshape(plane, token_rows, row_width // plane)
    )
    turns = [here ^ place for place in range(plane)]
    attended_grad = jnp.stack(
        [pick(attended_grad, turn // 2 + (plane // 2) * (turn % 2)) for turn in turns]
    )
    attended_grad = (
        attended_grad.reshape(plane, 2, half, 2, HEAD_DIM)
        .transpose(3, 1, 0, 2, 4)
        .reshape(PLANES, plane * half, HEAD_DIM)
    )
    arrived = jnp.stack(
        [
            lax.ppermute(pick(attended_grad, (level - step) % PLANES), "ctx", down[step])
            for step in range(PLANES)
        ]
    )
    grad_mine = jnp.concatenate(
        [pick(arrived, (tier - seat) % PLANES) for tier in range(PLANES)], axis=0
    ).reshape(peers, half, HEAD_DIM)
    grad_rows = jnp.concatenate([grad_mine, exchange(grad_mine)], axis=1).astype(jnp.float32)

    chosen = slot[:, :, None] == jnp.arange(slots, dtype=jnp.int32)
    log_by_source = log_slots.reshape(peers, peers, per_peer).transpose(1, 0, 2).reshape(peers, slots)
    log_own = jnp.sum(jnp.where(chosen, log_by_source[:, None, :], 0.0), axis=2)
    log_other = swapped(exchange(log_own))
    result_other = swapped(exchange(result))
    largest = jnp.maximum(log_own, log_other)
    lifted_own, lifted_other = jnp.exp(log_own - largest), jnp.exp(log_other - largest)
    lifted_sum = lifted_own + lifted_other
    weight_own, weight_other = lifted_own / lifted_sum, lifted_other / lifted_sum
    attended = (
        weight_own[:, :, None] * result.astype(jnp.float32)
        + weight_other[:, :, None] * result_other.astype(jnp.float32)
    ).astype(jnp.bfloat16)

    inner = jnp.sum(grad_rows * attended.astype(jnp.float32), axis=-1)
    shift = weight_own * inner
    query_grad = (weight_own[:, :, None] * grad_rows).astype(jnp.bfloat16)
    shift_slots = jnp.sum(jnp.where(chosen, shift[:, :, None], 0.0), axis=1)
    shift_slots = (
        shift_slots.reshape(peers, peers, per_peer).transpose(1, 0, 2).reshape(peers, slots)
    )

    attended_half = attended[:, :half].reshape(PLANES, plane * half, HEAD_DIM)
    arrived = jnp.stack(
        [
            lax.ppermute(
                pick(attended_half, (seat + step) % PLANES),
                "ctx",
                [(target, source) for source, target in down[step]],
            )
            for step in range(PLANES)
        ]
    )
    plane_attended = (
        jnp.stack([pick(arrived, (level - place) % PLANES) for place in range(PLANES)])
        .reshape(2, 2, plane, half, HEAD_DIM)
        .transpose(2, 1, 3, 0, 4)
        .reshape(plane, token_rows, row_width // plane)
    )
    parts = [pick(plane_attended, here ^ mask) for mask in masks]
    plane_attended = jnp.concatenate(parts, axis=0)
    landed = {
        mask: part if mask == 0 else moved(part, mask) for mask, part in zip(masks, parts)
    }
    landed = jnp.stack([landed[mask] for mask in range(plane)])
    attended_rows = jnp.concatenate([pick(landed, turn) for turn in turns], axis=1)

    attended_pair = jnp.concatenate([attended_rows, exchange(attended_rows)], axis=0)
    mixed_part = contract(attended_pair, half_weight, 1, 1).astype(jnp.bfloat16)
    mixed_kept, mixed_got = mixed_part[:token_rows], exchange(mixed_part[token_rows:])
    mixed_even = jnp.where(first, mixed_kept, mixed_got).reshape(token_rows, heads, 1, -1)
    mixed_odd = jnp.where(first, mixed_got, mixed_kept).reshape(token_rows, heads, 1, -1)
    mixed = jnp.concatenate([mixed_even, mixed_odd], axis=2).reshape(token_rows, row_width)

    partial = contract(plane_grad, plane_attended, 0, 0) * (1.0 / math.sqrt(token_rows * peers))
    partial = partial.astype(jnp.bfloat16).reshape(
        peers, row_width // peers, row_width // plane
    )
    query_grad, partial = lax.optimization_barrier((query_grad, partial))
    shares = everywhere(partial)
    shares = shares.reshape((PLANES, plane) + shares.shape[1:]).astype(jnp.float32)
    grad_weight = jnp.sum(shares, axis=0).transpose(1, 0, 2).reshape(-1, row_width)

    grads = kernel_call(
        backward_kernel,
        jax.ShapeDtypeStruct((peers, token_rows, 2 * HEAD_DIM), jnp.bfloat16),
        [
            pltpu.VMEM((peers, slots, 3 * HEAD_DIM), jnp.float32),
            pltpu.VMEM((peers, slots, 2 * HEAD_DIM), jnp.float32),
        ],
        (mine, other, query_grad, slot, code, log_slots, shift_slots),
    )
    grads_other = exchange(grads[:, half:])
    total = (grads[:, :half].astype(jnp.float32) + grads_other.astype(jnp.float32)).astype(
        jnp.bfloat16
    )
    back = everywhere(total)
    grad_qk = by_token(back[:, :, :HEAD_DIM])
    grad_values = by_token(back[:, :, HEAD_DIM:])

    return (mixed, grad_qk, grad_values, grad_weight)


def per_device(shared_qk, values, out_grad, out_weight, buckets):
    token_rows, row_width = shared_qk.shape
    peers = lax.axis_size("ctx")
    fits = (
        lax.axis_size("head") == 1
        and buckets.shape[0] == 2
        and peers == 2 * (row_width // HEAD_DIM)
        and 2 * token_rows == TALL
        and TALL // peers == 8
    )
    whole = head_owner_device if fits else bucket_owner_device
    return whole(shared_qk, values, out_grad, out_weight, buckets)


def solution(mesh):
    in_specs = (
        P("ctx", "head"),
        P("ctx", "head"),
        P("ctx", "head"),
        P("ctx", "head"),
        P(None, "ctx"),
    )
    out_specs = (P("ctx", "head"), P("ctx", "head"), P("ctx", "head"), P("ctx", "head"))
    return jax.shard_map(
        per_device, mesh=mesh, in_specs=in_specs, out_specs=out_specs, check_vma=False
    )
```

```python
import math

import jax
import jax.numpy as jnp
from jax import lax
from jax.experimental import pallas as pl
from jax.experimental.pallas import tpu as pltpu
from jax.sharding import PartitionSpec as P

HEAD_DIM = 128
SPAN = 128


self_penalty = 10000.0
masked_score = -1e30


def with_zero_row(matrix):
    return jnp.concatenate([matrix, jnp.zeros((1,) + matrix.shape[1:], matrix.dtype)], axis=0)


def key_windows(rows):
    row_count = rows.shape[0]
    leading = jnp.zeros((SPAN,) + rows.shape[1:], rows.dtype)
    earlier = jnp.concatenate([leading, rows[: row_count - SPAN]], axis=0)
    shape_out = (row_count // SPAN, SPAN) + rows.shape[1:]
    return jnp.concatenate([earlier.reshape(shape_out), rows.reshape(shape_out)], axis=1)


def fold_windows(stacked):
    current = stacked[:, SPAN:]
    earlier = stacked[:, :SPAN]
    return current + jnp.concatenate([earlier[1:], jnp.zeros_like(earlier[:1])], axis=0)


def span_probs(queries, key_rows, key_live):
    scores = jnp.einsum(
        "qhd,khd->hqk", queries, key_rows, preferred_element_type=jnp.float32
    ) * HEAD_DIM ** (-0.5)
    itself = jnp.arange(2 * SPAN)[None, :] == jnp.arange(SPAN)[:, None] + SPAN
    scores = jnp.where(itself[None], scores - self_penalty, scores)
    scores = jnp.where(key_live[None, None, :], scores, masked_score)
    largest = jnp.max(scores, axis=-1, keepdims=True)
    lifted = jnp.exp(scores - largest)
    summed = jnp.sum(lifted, axis=-1, keepdims=True)
    return (lifted / summed, (largest + jnp.log(summed))[..., 0])


def owner_forward(own_qk, own_values, occupied, local_heads):
    blocks = own_qk.shape[0] // SPAN
    queries = own_qk.reshape(blocks, SPAN, local_heads, HEAD_DIM)
    key_rows = key_windows(own_qk).reshape(blocks, 2 * SPAN, local_heads, HEAD_DIM)
    value_rows = key_windows(own_values).reshape(blocks, 2 * SPAN, local_heads, HEAD_DIM)
    live_keys = key_windows(occupied)

    def one_block(pieces):
        block_query, block_key, block_value, block_live = pieces
        probability, log_total = span_probs(block_query, block_key, block_live)
        result = jnp.einsum(
            "hqk,khd->qhd",
            probability.astype(jnp.bfloat16),
            block_value,
            preferred_element_type=jnp.float32,
        )
        return (result.astype(jnp.bfloat16).reshape(SPAN, local_heads * HEAD_DIM), log_total.T)

    outputs, log_totals = lax.map(one_block, (queries, key_rows, value_rows, live_keys))
    return (outputs.reshape(-1, local_heads * HEAD_DIM), log_totals.reshape(-1, local_heads))


def owner_backward(own_qk, own_values, occupied, own_grad, own_shift, local_heads):
    blocks = own_qk.shape[0] // SPAN
    queries = own_qk.reshape(blocks, SPAN, local_heads, HEAD_DIM)
    key_rows = key_windows(own_qk).reshape(blocks, 2 * SPAN, local_heads, HEAD_DIM)
    value_rows = key_windows(own_values).reshape(blocks, 2 * SPAN, local_heads, HEAD_DIM)
    live_keys = key_windows(occupied)
    grad_rows = own_grad.reshape(blocks, SPAN, local_heads, HEAD_DIM)
    shift_rows = own_shift.reshape(blocks, SPAN, local_heads)

    def one_block(pieces):
        block_query, block_key, block_value, block_live, block_grad, block_shift = pieces
        probability, log_total = span_probs(block_query, block_key, block_live)
        prob_grad = jnp.einsum(
            "qhd,khd->hqk", block_grad, block_value, preferred_element_type=jnp.float32
        )
        score_grad = (probability * (prob_grad - block_shift.T[:, :, None])).astype(jnp.bfloat16)
        query_grad = jnp.einsum(
            "hqk,khd->qhd", score_grad, block_key, preferred_element_type=jnp.float32
        ) * HEAD_DIM ** (-0.5)
        key_grad = jnp.einsum(
            "hqk,qhd->khd", score_grad, block_query, preferred_element_type=jnp.float32
        ) * HEAD_DIM ** (-0.5)
        value_grad = jnp.einsum(
            "hqk,qhd->khd",
            probability.astype(jnp.bfloat16),
            block_grad,
            preferred_element_type=jnp.float32,
        )
        return (query_grad, key_grad, value_grad)

    query_grad, key_grad, value_grad = lax.map(
        one_block, (queries, key_rows, value_rows, live_keys, grad_rows, shift_rows)
    )
    row_width = local_heads * HEAD_DIM
    qk_rows = (query_grad + fold_windows(key_grad)).reshape(-1, row_width).astype(jnp.bfloat16)
    value_out = fold_windows(value_grad).reshape(-1, row_width).astype(jnp.bfloat16)
    return (qk_rows, value_out)


def route_round(bucket_row, peer_count, per_peer, token_rows):
    owners = jnp.arange(peer_count, dtype=jnp.int32)
    member = (bucket_row[:, None] == owners[None, :]).astype(jnp.int32)
    earlier = jnp.cumsum(member, axis=0) - member
    position = jnp.sum(earlier * member, axis=1)
    slot_index = bucket_row * per_peer + position
    slot_token = (
        jnp.full((peer_count * per_peer,), token_rows, jnp.int32)
        .at[slot_index]
        .set(jnp.arange(token_rows, dtype=jnp.int32))
    )
    return (slot_index, slot_token)


def compact_slots(slot_marks, capacity):
    target = jnp.cumsum(slot_marks) - 1
    target = jnp.where(slot_marks > 0, target, capacity).astype(jnp.int32)
    source_slot = (
        jnp.full((capacity,), capacity, jnp.int32)
        .at[target]
        .set(jnp.arange(capacity, dtype=jnp.int32), mode="drop")
    )
    return (source_slot, target)


def bucket_owner_device(shared_qk, values, out_grad, out_weight, buckets):
    token_rows, row_width = shared_qk.shape
    local_heads = row_width // HEAD_DIM
    peer_count = lax.axis_size("ctx")
    capacity = 2 * token_rows
    per_peer = capacity // peer_count
    rounds = buckets.shape[0]
    routes = [
        route_round(buckets[round_index], peer_count, per_peer, token_rows)
        for round_index in range(rounds)
    ]
    padded_qk = with_zero_row(shared_qk)
    padded_values = with_zero_row(values)
    whole_weight = lax.all_gather(out_weight, "ctx", axis=0, tiled=True)
    groups = [[round_index] for round_index in range(rounds)]

    def outgoing(matrix, round_index):
        return matrix[routes[round_index][1]].reshape((peer_count, per_peer) + matrix.shape[1:])

    def homeward(received, round_index):
        flat_rows = received.reshape((peer_count * per_peer,) + received.shape[2:])
        return flat_rows[routes[round_index][0]]

    round_outputs = [None] * rounds
    round_logs = [None] * rounds
    owner_state = [None] * rounds
    for round_group in groups:
        send_qk = jnp.stack(
            [outgoing(padded_qk, round_index) for round_index in round_group], axis=1
        )
        send_values = jnp.stack(
            [outgoing(padded_values, round_index) for round_index in round_group], axis=1
        )
        slot_marks = jnp.stack(
            [
                (routes[round_index][1] < token_rows)
                .astype(jnp.int32)
                .reshape(peer_count, per_peer)
                for round_index in round_group
            ],
            axis=1,
        )
        got_qk, got_values, got_marks = (
            lax.all_to_all(send_qk, "ctx", split_axis=0, concat_axis=0, tiled=True),
            lax.all_to_all(send_values, "ctx", split_axis=0, concat_axis=0, tiled=True),
            lax.all_to_all(slot_marks, "ctx", split_axis=0, concat_axis=0, tiled=True),
        )
        returned_rows = []
        returned_logs = []
        for member_index, round_index in enumerate(round_group):
            source_slot, target = compact_slots(got_marks[:, member_index].reshape(-1), capacity)
            own_qk = with_zero_row(got_qk[:, member_index].reshape(capacity, row_width))[
                source_slot
            ]
            own_values = with_zero_row(got_values[:, member_index].reshape(capacity, row_width))[
                source_slot
            ]
            occupied = source_slot < capacity
            rows_out, logs_out = owner_forward(own_qk, own_values, occupied, local_heads)
            owner_state[round_index] = (own_qk, own_values, occupied, source_slot, target)
            returned_rows.append(
                with_zero_row(rows_out)[target].reshape(peer_count, per_peer, row_width)
            )
            returned_logs.append(
                with_zero_row(logs_out)[target].reshape(peer_count, per_peer, local_heads)
            )
        back_rows, back_logs = (
            lax.all_to_all(
                jnp.stack(returned_rows, axis=1).astype(jnp.float32),
                "ctx",
                split_axis=0,
                concat_axis=0,
                tiled=True,
            ).astype(jnp.bfloat16),
            lax.all_to_all(
                jnp.stack(returned_logs, axis=1), "ctx", split_axis=0, concat_axis=0, tiled=True
            ),
        )
        for member_index, round_index in enumerate(round_group):
            round_outputs[round_index] = homeward(back_rows[:, member_index], round_index)
            round_logs[round_index] = homeward(back_logs[:, member_index], round_index)
    log_stack = jnp.stack(round_logs)
    largest = jnp.max(log_stack, axis=0)
    lifted = jnp.exp(log_stack - largest)
    round_weight = lifted / jnp.sum(lifted, axis=0)
    row_stack = (
        jnp.stack(round_outputs)
        .astype(jnp.float32)
        .reshape(rounds, token_rows, local_heads, HEAD_DIM)
    )
    attended = (
        jnp.sum(round_weight[..., None] * row_stack, axis=0)
        .reshape(token_rows, row_width)
        .astype(jnp.bfloat16)
    )
    partial_value = lax.dot_general(
        attended, whole_weight, (((1,), (1,)), ((), ())), preferred_element_type=jnp.float32
    )
    mixed = lax.psum_scatter(partial_value, "head", scatter_dimension=1, tiled=True).astype(
        jnp.bfloat16
    )
    full_grad = lax.all_gather(out_grad, "head", axis=1, tiled=True)
    attended_grad = jnp.dot(full_grad, whole_weight, preferred_element_type=jnp.float32)
    token_total = token_rows * peer_count
    grad_weight = lax.psum_scatter(
        lax.dot_general(
            full_grad, attended, (((0,), (0,)), ((), ())), preferred_element_type=jnp.float32
        ),
        "ctx",
        scatter_dimension=0,
        tiled=True,
    ) * (1.0 / math.sqrt(token_total))
    grad_heads = attended_grad.reshape(token_rows, local_heads, HEAD_DIM)
    inner = jnp.sum(
        grad_heads * attended.astype(jnp.float32).reshape(token_rows, local_heads, HEAD_DIM),
        axis=-1,
    )
    qk_total = jnp.zeros((token_rows, row_width), jnp.float32)
    value_total = jnp.zeros((token_rows, row_width), jnp.float32)
    for round_group in groups:
        send_grad = jnp.stack(
            [
                outgoing(
                    with_zero_row(
                        (round_weight[round_index][..., None] * grad_heads)
                        .reshape(token_rows, row_width)
                        .astype(jnp.bfloat16)
                    ),
                    round_index,
                )
                for round_index in round_group
            ],
            axis=1,
        )
        send_shift = jnp.stack(
            [
                outgoing(with_zero_row(round_weight[round_index] * inner), round_index)
                for round_index in round_group
            ],
            axis=1,
        )
        got_grad, got_shift = (
            lax.all_to_all(
                send_grad.astype(jnp.float32), "ctx", split_axis=0, concat_axis=0, tiled=True
            ).astype(send_grad.dtype),
            lax.all_to_all(send_shift, "ctx", split_axis=0, concat_axis=0, tiled=True),
        )
        returned_qk = []
        returned_values = []
        for member_index, round_index in enumerate(round_group):
            own_qk, own_values, occupied, source_slot, target = owner_state[round_index]
            own_grad = with_zero_row(got_grad[:, member_index].reshape(capacity, row_width))[
                source_slot
            ]
            own_shift = with_zero_row(got_shift[:, member_index].reshape(capacity, local_heads))[
                source_slot
            ]
            qk_rows, value_rows = owner_backward(
                own_qk, own_values, occupied, own_grad, own_shift, local_heads
            )
            returned_qk.append(
                with_zero_row(qk_rows)[target].reshape(peer_count, per_peer, row_width)
            )
            returned_values.append(
                with_zero_row(value_rows)[target].reshape(peer_count, per_peer, row_width)
            )
        back_qk, back_values = (
            lax.all_to_all(
                jnp.stack(returned_qk, axis=1), "ctx", split_axis=0, concat_axis=0, tiled=True
            ),
            lax.all_to_all(
                jnp.stack(returned_values, axis=1), "ctx", split_axis=0, concat_axis=0, tiled=True
            ),
        )
        for member_index, round_index in enumerate(round_group):
            qk_total = qk_total + homeward(back_qk[:, member_index], round_index).astype(
                jnp.float32
            )
            value_total = value_total + homeward(back_values[:, member_index], round_index).astype(
                jnp.float32
            )
    return (mixed, qk_total.astype(jnp.bfloat16), value_total.astype(jnp.bfloat16), grad_weight)


PLANES = 4
TALL = 256
HALF = 64
VMEM_BYTES = 48 * 1024 * 1024


def contract(left, right, left_dim, right_dim):
    return lax.dot_general(
        left, right, (((left_dim,), (right_dim,)), ((), ())), preferred_element_type=jnp.float32
    )


def slot_pick(slot_ref, source):
    slot_ids = lax.broadcasted_iota(jnp.int32, (TALL, SPAN), 0)
    return (slot_ids == slot_ref[pl.ds(source, 1), :]).astype(jnp.bfloat16)


def bucket_scores(rows, code_ref, bucket):
    scores = contract(rows, rows, 1, 1) * HEAD_DIM ** (-0.5)
    key_ids = lax.broadcasted_iota(jnp.int32, (TALL, TALL), 0)
    query_ids = lax.broadcasted_iota(jnp.int32, (TALL, TALL), 1)
    scores = jnp.where(key_ids == query_ids, scores - self_penalty, scores)
    code_row = code_ref[pl.ds(bucket, 1), :]
    code_column = jnp.broadcast_to(code_row, (SPAN, TALL)).T
    code_column = jnp.concatenate([code_column, code_column], axis=1)
    seen = (code_column > 0.5) & (code_column <= jnp.maximum(code_row, 1.0))
    return jnp.where(seen, scores, masked_score)


def forward_kernel(mine_ref, other_ref, slot_ref, code_ref, out_ref, log_ref, grouped, results):
    sources, slots = grouped.shape[0], grouped.shape[1]
    per_peer = TALL // sources
    buckets = slots // per_peer

    def group(source, carry):
        rows = jnp.concatenate([mine_ref[source, :HALF], other_ref[source]], axis=0)
        grouped[source] = contract(slot_pick(slot_ref, source), rows, 1, 0)
        return carry

    lax.fori_loop(0, sources, group, 0, unroll=2)

    def attend(bucket, carry):
        place = pl.ds(pl.multiple_of(bucket * per_peer, per_peer), per_peer)
        rows = grouped[:, place, :].reshape(TALL, 2 * HEAD_DIM).astype(jnp.bfloat16)
        scores = bucket_scores(rows[:, :HEAD_DIM], code_ref, bucket)
        largest = jnp.max(scores, axis=0, keepdims=True)
        lifted = jnp.exp(scores - largest)
        summed = jnp.sum(lifted, axis=0, keepdims=True)
        probability = (lifted / summed).astype(jnp.bfloat16)
        result = contract(probability, rows[:, HEAD_DIM:], 0, 0)
        results[:, place, :] = result.reshape(sources, per_peer, HEAD_DIM)
        log_ref[pl.ds(bucket, 1), :] = largest + jnp.log(summed)
        return carry

    lax.fori_loop(0, buckets, attend, 0, unroll=2)

    def scatter(source, carry):
        rows = results[source].astype(jnp.bfloat16)
        out_ref[source] = contract(slot_pick(slot_ref, source), rows, 0, 0).astype(jnp.bfloat16)
        return carry

    lax.fori_loop(0, sources, scatter, 0, unroll=2)


def backward_kernel(
    mine_ref, other_ref, grad_ref, slot_ref, code_ref, log_ref, shift_ref, out_ref, grouped, results
):
    sources, slots = grouped.shape[0], grouped.shape[1]
    per_peer = TALL // sources
    buckets = slots // per_peer
    both = 2 * HEAD_DIM

    def group(source, carry):
        rows = jnp.concatenate([mine_ref[source, :HALF], other_ref[source]], axis=0)
        pick = slot_pick(slot_ref, source)
        grouped[source, :, :both] = contract(pick, rows, 1, 0)
        grouped[source, :, both:] = contract(pick, grad_ref[source], 1, 0)
        return carry

    lax.fori_loop(0, sources, group, 0, unroll=2)

    def attend(bucket, carry):
        place = pl.ds(pl.multiple_of(bucket * per_peer, per_peer), per_peer)
        rows = grouped[:, place, :].reshape(TALL, 3 * HEAD_DIM).astype(jnp.bfloat16)
        qk_rows, value_rows, grad_rows = (
            rows[:, :HEAD_DIM],
            rows[:, HEAD_DIM:both],
            rows[:, both:],
        )
        scores = bucket_scores(qk_rows, code_ref, bucket)
        probability = jnp.exp(scores - log_ref[pl.ds(bucket, 1), :])
        prob_grad = contract(value_rows, grad_rows, 1, 1)
        score_grad = (probability * (prob_grad - shift_ref[pl.ds(bucket, 1), :])).astype(
            jnp.bfloat16
        )
        qk_grad = contract(score_grad, qk_rows, 0, 0) + contract(score_grad, qk_rows, 1, 0)
        value_grad = contract(probability.astype(jnp.bfloat16), grad_rows, 1, 0)
        results[:, place, :HEAD_DIM] = (qk_grad * HEAD_DIM ** (-0.5)).reshape(
            sources, per_peer, HEAD_DIM
        )
        results[:, place, HEAD_DIM:] = value_grad.reshape(sources, per_peer, HEAD_DIM)
        return carry

    lax.fori_loop(0, buckets, attend, 0, unroll=2)

    def scatter(source, carry):
        rows = results[source].astype(jnp.bfloat16)
        out_ref[source] = contract(slot_pick(slot_ref, source), rows, 0, 0).astype(jnp.bfloat16)
        return carry

    lax.fori_loop(0, sources, scatter, 0, unroll=2)


def kernel_call(body, out_shape, scratch_shapes, arguments):
    return pl.pallas_call(
        body,
        out_shape=out_shape,
        in_specs=[pl.BlockSpec(memory_space=pltpu.VMEM)] * len(arguments),
        out_specs=jax.tree.map(lambda _: pl.BlockSpec(memory_space=pltpu.VMEM), out_shape),
        scratch_shapes=scratch_shapes,
        compiler_params=pltpu.CompilerParams(vmem_limit_bytes=VMEM_BYTES),
    )(*arguments)


def head_owner_device(shared_qk, values, out_grad, out_weight, buckets):
    token_rows, row_width = shared_qk.shape
    heads = row_width // HEAD_DIM
    peers = lax.axis_size("ctx")
    per_peer = 2 * token_rows // peers
    half = token_rows // 2
    slots = peers * per_peer
    core = lax.axis_index("ctx") % 2
    first = core == 0
    partners = [(device, device ^ 1) for device in range(peers)]

    def exchange(block):
        return lax.ppermute(block, "ctx", partners)

    def swapped(block):
        return jnp.concatenate([block[:, half:], block[:, :half]], axis=1)

    def everywhere(block):
        return lax.all_to_all(block, "ctx", split_axis=0, concat_axis=0, tiled=True)

    def by_head(rows):
        return rows.reshape(2, half, heads, HEAD_DIM).transpose(2, 0, 1, 3)

    def by_token(blocks):
        return blocks.reshape(heads, 2, half, HEAD_DIM).transpose(1, 2, 0, 3).reshape(
            token_rows, row_width
        )

    def own_half(rows):
        parted = rows.reshape(rows.shape[0], heads, 2, -1)
        even, odd = parted[:, :, 0], parted[:, :, 1]
        kept, passed = jnp.where(first, even, odd), jnp.where(first, odd, even)
        return kept.reshape(rows.shape[0], -1), passed.reshape(rows.shape[0], -1)

    plane = peers // PLANES
    index = lax.axis_index("ctx")
    level, here, seat = index // plane, index % plane, index % PLANES
    up = [
        [
            (PLANES * place + (tier - step) % PLANES, tier * plane + place)
            for tier in range(PLANES)
            for place in range(plane)
        ]
        for step in range(PLANES)
    ]

    def pick(blocks, which):
        return lax.dynamic_index_in_dim(blocks, which, axis=0, keepdims=False)

    def moved(block, mask):
        return lax.ppermute(block, "ctx", [(device, device ^ mask) for device in range(peers)])

    half_weight = lax.all_gather(
        out_weight,
        "ctx",
        axis=0,
        tiled=True,
        axis_index_groups=[list(range(0, peers, 2)), list(range(1, peers, 2))],
    )

    tag = jnp.pad(buckets.astype(jnp.bfloat16).reshape(1, -1), ((0, 7), (0, 0)))
    sent = jnp.concatenate([by_head(shared_qk), by_head(values)], axis=-1)
    sent = jnp.concatenate(
        [
            sent.reshape(peers, half, 2 * HEAD_DIM),
            jnp.broadcast_to(tag[None], (peers, 8, 2 * HEAD_DIM)),
        ],
        axis=1,
    )
    mine = everywhere(sent)
    other = exchange(mine[:, :half])

    all_buckets = mine[:, half].astype(jnp.int32).reshape(peers, 2, token_rows)
    own = jnp.where(first, all_buckets[:, 0], all_buckets[:, 1])
    order = jnp.arange(token_rows, dtype=jnp.int32)
    same = (own[:, :, None] == own[:, None, :]) & (order[None, :] < order[:, None])[None]
    position = jnp.sum(same.astype(jnp.int32), axis=2)
    slot = own * per_peer + position
    slot = jnp.where(first, slot, swapped(slot))
    bucket_ids = jnp.arange(peers, dtype=jnp.int32)
    counts = jnp.sum((own[:, :, None] == bucket_ids).astype(jnp.int32), axis=1)
    before = (bucket_ids[None, :] < bucket_ids[:, None]).astype(jnp.int32)
    starts = jnp.sum(before[:, :, None] * counts[None], axis=1)
    within = jnp.arange(per_peer, dtype=jnp.int32)
    live = within < counts[:, :, None]
    code = jnp.where(live, jnp.where(starts[:, :, None] + within >= SPAN, 2.0, 1.0), 0.0)
    code = code.astype(jnp.float32).transpose(1, 0, 2).reshape(peers, peers * per_peer)

    result, log_slots = kernel_call(
        forward_kernel,
        (
            jax.ShapeDtypeStruct((peers, token_rows, HEAD_DIM), jnp.bfloat16),
            jax.ShapeDtypeStruct((peers, peers * per_peer), jnp.float32),
        ),
        [
            pltpu.VMEM((peers, slots, 2 * HEAD_DIM), jnp.float32),
            pltpu.VMEM((peers, slots, HEAD_DIM), jnp.float32),
        ],
        (mine, other, slot, code),
    )

    grad_kept, grad_passed = own_half(out_grad)
    grad_pair = jnp.concatenate([grad_kept, exchange(grad_passed)], axis=0)
    grad_pair, result, log_slots = lax.optimization_barrier((grad_pair, result, log_slots))
    grad_part = jnp.dot(grad_pair, half_weight, preferred_element_type=jnp.float32)
    attended_grad = (grad_part[:token_rows] + exchange(grad_part[token_rows:])).astype(
        jnp.bfloat16
    )
    grad_mine = everywhere(by_head(attended_grad).reshape(peers, half, HEAD_DIM))
    grad_rows = jnp.concatenate([grad_mine, exchange(grad_mine)], axis=1).astype(jnp.float32)

    chosen = slot[:, :, None] == jnp.arange(slots, dtype=jnp.int32)
    log_by_source = log_slots.reshape(peers, peers, per_peer).transpose(1, 0, 2).reshape(peers, slots)
    log_own = jnp.sum(jnp.where(chosen, log_by_source[:, None, :], 0.0), axis=2)
    log_other = swapped(exchange(log_own))
    result_other = swapped(exchange(result))
    largest = jnp.maximum(log_own, log_other)
    lifted_own, lifted_other = jnp.exp(log_own - largest), jnp.exp(log_other - largest)
    lifted_sum = lifted_own + lifted_other
    weight_own, weight_other = lifted_own / lifted_sum, lifted_other / lifted_sum
    attended = (
        weight_own[:, :, None] * result.astype(jnp.float32)
        + weight_other[:, :, None] * result_other.astype(jnp.float32)
    ).astype(jnp.bfloat16)

    inner = jnp.sum(grad_rows * attended.astype(jnp.float32), axis=-1)
    shift = weight_own * inner
    query_grad = (weight_own[:, :, None] * grad_rows).astype(jnp.bfloat16)
    shift_slots = jnp.sum(jnp.where(chosen, shift[:, :, None], 0.0), axis=1)
    shift_slots = (
        shift_slots.reshape(peers, peers, per_peer).transpose(1, 0, 2).reshape(peers, slots)
    )

    attended_rows = by_token(everywhere(attended[:, :half]))

    attended_pair = jnp.concatenate([attended_rows, exchange(attended_rows)], axis=0)
    mixed_part = contract(attended_pair, half_weight, 1, 1).astype(jnp.bfloat16)
    mixed_kept, mixed_got = mixed_part[:token_rows], exchange(mixed_part[token_rows:])
    mixed_even = jnp.where(first, mixed_kept, mixed_got).reshape(token_rows, heads, 1, -1)
    mixed_odd = jnp.where(first, mixed_got, mixed_kept).reshape(token_rows, heads, 1, -1)
    mixed = jnp.concatenate([mixed_even, mixed_odd], axis=2).reshape(token_rows, row_width)

    attended_half = attended[:, :half].reshape(PLANES, plane * half, HEAD_DIM)
    arrived = jnp.stack(
        [
            lax.ppermute(pick(attended_half, (seat + step) % PLANES), "ctx", up[step])
            for step in range(PLANES)
        ]
    )
    plane_attended = (
        jnp.stack([pick(arrived, (level - place) % PLANES) for place in range(PLANES)])
        .reshape(2, 2, plane, half, HEAD_DIM)
        .transpose(2, 1, 3, 0, 4)
        .reshape(plane, token_rows, row_width // plane)
    )
    plane_attended = jnp.concatenate(
        [pick(plane_attended, here ^ mask) for mask in (0, 2, 4, 6, 1, 3, 5, 7)], axis=0
    )
    left, right = out_grad[:, : row_width // 2], out_grad[:, row_width // 2 :]
    left_two = jnp.concatenate([left, moved(left, 2)], axis=0)
    right_x = moved(right, 4)
    right_two = jnp.concatenate([right, right_x], axis=0)
    left_four = jnp.concatenate([left_two, moved(left_two, 4)], axis=0)
    right_far = moved(right_two, 2)
    right_four = jnp.concatenate(
        [right, right_far[:token_rows], right_x, right_far[token_rows:]], axis=0
    )
    core_grad = jnp.concatenate([left_four, right_four], axis=1)
    plane_grad = jnp.concatenate([core_grad, exchange(core_grad)], axis=0)
    partial = contract(plane_grad, plane_attended, 0, 0) * (1.0 / math.sqrt(token_rows * peers))
    partial = partial.astype(jnp.bfloat16).reshape(
        peers, row_width // peers, row_width // plane
    )
    query_grad, partial = lax.optimization_barrier((query_grad, partial))
    shares = everywhere(partial)
    shares = shares.reshape((PLANES, plane) + shares.shape[1:]).astype(jnp.float32)
    grad_weight = jnp.sum(shares, axis=0).transpose(1, 0, 2).reshape(-1, row_width)

    grads = kernel_call(
        backward_kernel,
        jax.ShapeDtypeStruct((peers, token_rows, 2 * HEAD_DIM), jnp.bfloat16),
        [
            pltpu.VMEM((peers, slots, 3 * HEAD_DIM), jnp.float32),
            pltpu.VMEM((peers, slots, 2 * HEAD_DIM), jnp.float32),
        ],
        (mine, other, query_grad, slot, code, log_slots, shift_slots),
    )
    grads_other = exchange(grads[:, half:])
    total = (grads[:, :half].astype(jnp.float32) + grads_other.astype(jnp.float32)).astype(
        jnp.bfloat16
    )
    back = everywhere(total)
    grad_qk = by_token(back[:, :, :HEAD_DIM])
    grad_values = by_token(back[:, :, HEAD_DIM:])

    return (mixed, grad_qk, grad_values, grad_weight)


def per_device(shared_qk, values, out_grad, out_weight, buckets):
    token_rows, row_width = shared_qk.shape
    peers = lax.axis_size("ctx")
    fits = (
        lax.axis_size("head") == 1
        and buckets.shape[0] == 2
        and peers == 2 * (row_width // HEAD_DIM)
        and 2 * token_rows == TALL
        and TALL // peers == 8
    )
    whole = head_owner_device if fits else bucket_owner_device
    return whole(shared_qk, values, out_grad, out_weight, buckets)


def solution(mesh):
    in_specs = (
        P("ctx", "head"),
        P("ctx", "head"),
        P("ctx", "head"),
        P("ctx", "head"),
        P(None, "ctx"),
    )
    out_specs = (P("ctx", "head"), P("ctx", "head"), P("ctx", "head"), P("ctx", "head"))
    return jax.shard_map(
        per_device, mesh=mesh, in_specs=in_specs, out_specs=out_specs, check_vma=False
    )
```

```python
import math

import jax
import jax.numpy as jnp
from jax import lax
from jax.experimental import pallas as pl
from jax.experimental.pallas import tpu as pltpu
from jax.sharding import PartitionSpec as P

HEAD_DIM = 128
SPAN = 128


self_penalty = 10000.0
masked_score = -1e30


def with_zero_row(matrix):
    return jnp.concatenate([matrix, jnp.zeros((1,) + matrix.shape[1:], matrix.dtype)], axis=0)


def key_windows(rows):
    row_count = rows.shape[0]
    leading = jnp.zeros((SPAN,) + rows.shape[1:], rows.dtype)
    earlier = jnp.concatenate([leading, rows[: row_count - SPAN]], axis=0)
    shape_out = (row_count // SPAN, SPAN) + rows.shape[1:]
    return jnp.concatenate([earlier.reshape(shape_out), rows.reshape(shape_out)], axis=1)


def fold_windows(stacked):
    current = stacked[:, SPAN:]
    earlier = stacked[:, :SPAN]
    return current + jnp.concatenate([earlier[1:], jnp.zeros_like(earlier[:1])], axis=0)


def span_probs(queries, key_rows, key_live):
    scores = jnp.einsum(
        "qhd,khd->hqk", queries, key_rows, preferred_element_type=jnp.float32
    ) * HEAD_DIM ** (-0.5)
    itself = jnp.arange(2 * SPAN)[None, :] == jnp.arange(SPAN)[:, None] + SPAN
    scores = jnp.where(itself[None], scores - self_penalty, scores)
    scores = jnp.where(key_live[None, None, :], scores, masked_score)
    largest = jnp.max(scores, axis=-1, keepdims=True)
    lifted = jnp.exp(scores - largest)
    summed = jnp.sum(lifted, axis=-1, keepdims=True)
    return (lifted / summed, (largest + jnp.log(summed))[..., 0])


def owner_forward(own_qk, own_values, occupied, local_heads):
    blocks = own_qk.shape[0] // SPAN
    queries = own_qk.reshape(blocks, SPAN, local_heads, HEAD_DIM)
    key_rows = key_windows(own_qk).reshape(blocks, 2 * SPAN, local_heads, HEAD_DIM)
    value_rows = key_windows(own_values).reshape(blocks, 2 * SPAN, local_heads, HEAD_DIM)
    live_keys = key_windows(occupied)

    def one_block(pieces):
        block_query, block_key, block_value, block_live = pieces
        probability, log_total = span_probs(block_query, block_key, block_live)
        result = jnp.einsum(
            "hqk,khd->qhd",
            probability.astype(jnp.bfloat16),
            block_value,
            preferred_element_type=jnp.float32,
        )
        return (result.astype(jnp.bfloat16).reshape(SPAN, local_heads * HEAD_DIM), log_total.T)

    outputs, log_totals = lax.map(one_block, (queries, key_rows, value_rows, live_keys))
    return (outputs.reshape(-1, local_heads * HEAD_DIM), log_totals.reshape(-1, local_heads))


def owner_backward(own_qk, own_values, occupied, own_grad, own_shift, local_heads):
    blocks = own_qk.shape[0] // SPAN
    queries = own_qk.reshape(blocks, SPAN, local_heads, HEAD_DIM)
    key_rows = key_windows(own_qk).reshape(blocks, 2 * SPAN, local_heads, HEAD_DIM)
    value_rows = key_windows(own_values).reshape(blocks, 2 * SPAN, local_heads, HEAD_DIM)
    live_keys = key_windows(occupied)
    grad_rows = own_grad.reshape(blocks, SPAN, local_heads, HEAD_DIM)
    shift_rows = own_shift.reshape(blocks, SPAN, local_heads)

    def one_block(pieces):
        block_query, block_key, block_value, block_live, block_grad, block_shift = pieces
        probability, log_total = span_probs(block_query, block_key, block_live)
        prob_grad = jnp.einsum(
            "qhd,khd->hqk", block_grad, block_value, preferred_element_type=jnp.float32
        )
        score_grad = (probability * (prob_grad - block_shift.T[:, :, None])).astype(jnp.bfloat16)
        query_grad = jnp.einsum(
            "hqk,khd->qhd", score_grad, block_key, preferred_element_type=jnp.float32
        ) * HEAD_DIM ** (-0.5)
        key_grad = jnp.einsum(
            "hqk,qhd->khd", score_grad, block_query, preferred_element_type=jnp.float32
        ) * HEAD_DIM ** (-0.5)
        value_grad = jnp.einsum(
            "hqk,qhd->khd",
            probability.astype(jnp.bfloat16),
            block_grad,
            preferred_element_type=jnp.float32,
        )
        return (query_grad, key_grad, value_grad)

    query_grad, key_grad, value_grad = lax.map(
        one_block, (queries, key_rows, value_rows, live_keys, grad_rows, shift_rows)
    )
    row_width = local_heads * HEAD_DIM
    qk_rows = (query_grad + fold_windows(key_grad)).reshape(-1, row_width).astype(jnp.bfloat16)
    value_out = fold_windows(value_grad).reshape(-1, row_width).astype(jnp.bfloat16)
    return (qk_rows, value_out)


def route_round(bucket_row, peer_count, per_peer, token_rows):
    owners = jnp.arange(peer_count, dtype=jnp.int32)
    member = (bucket_row[:, None] == owners[None, :]).astype(jnp.int32)
    earlier = jnp.cumsum(member, axis=0) - member
    position = jnp.sum(earlier * member, axis=1)
    slot_index = bucket_row * per_peer + position
    slot_token = (
        jnp.full((peer_count * per_peer,), token_rows, jnp.int32)
        .at[slot_index]
        .set(jnp.arange(token_rows, dtype=jnp.int32))
    )
    return (slot_index, slot_token)


def compact_slots(slot_marks, capacity):
    target = jnp.cumsum(slot_marks) - 1
    target = jnp.where(slot_marks > 0, target, capacity).astype(jnp.int32)
    source_slot = (
        jnp.full((capacity,), capacity, jnp.int32)
        .at[target]
        .set(jnp.arange(capacity, dtype=jnp.int32), mode="drop")
    )
    return (source_slot, target)


def bucket_owner_device(shared_qk, values, out_grad, out_weight, buckets):
    token_rows, row_width = shared_qk.shape
    local_heads = row_width // HEAD_DIM
    peer_count = lax.axis_size("ctx")
    capacity = 2 * token_rows
    per_peer = capacity // peer_count
    rounds = buckets.shape[0]
    routes = [
        route_round(buckets[round_index], peer_count, per_peer, token_rows)
        for round_index in range(rounds)
    ]
    padded_qk = with_zero_row(shared_qk)
    padded_values = with_zero_row(values)
    whole_weight = lax.all_gather(out_weight, "ctx", axis=0, tiled=True)
    groups = [[round_index] for round_index in range(rounds)]

    def outgoing(matrix, round_index):
        return matrix[routes[round_index][1]].reshape((peer_count, per_peer) + matrix.shape[1:])

    def homeward(received, round_index):
        flat_rows = received.reshape((peer_count * per_peer,) + received.shape[2:])
        return flat_rows[routes[round_index][0]]

    round_outputs = [None] * rounds
    round_logs = [None] * rounds
    owner_state = [None] * rounds
    for round_group in groups:
        send_qk = jnp.stack(
            [outgoing(padded_qk, round_index) for round_index in round_group], axis=1
        )
        send_values = jnp.stack(
            [outgoing(padded_values, round_index) for round_index in round_group], axis=1
        )
        slot_marks = jnp.stack(
            [
                (routes[round_index][1] < token_rows)
                .astype(jnp.int32)
                .reshape(peer_count, per_peer)
                for round_index in round_group
            ],
            axis=1,
        )
        got_qk, got_values, got_marks = (
            lax.all_to_all(send_qk, "ctx", split_axis=0, concat_axis=0, tiled=True),
            lax.all_to_all(send_values, "ctx", split_axis=0, concat_axis=0, tiled=True),
            lax.all_to_all(slot_marks, "ctx", split_axis=0, concat_axis=0, tiled=True),
        )
        returned_rows = []
        returned_logs = []
        for member_index, round_index in enumerate(round_group):
            source_slot, target = compact_slots(got_marks[:, member_index].reshape(-1), capacity)
            own_qk = with_zero_row(got_qk[:, member_index].reshape(capacity, row_width))[
                source_slot
            ]
            own_values = with_zero_row(got_values[:, member_index].reshape(capacity, row_width))[
                source_slot
            ]
            occupied = source_slot < capacity
            rows_out, logs_out = owner_forward(own_qk, own_values, occupied, local_heads)
            owner_state[round_index] = (own_qk, own_values, occupied, source_slot, target)
            returned_rows.append(
                with_zero_row(rows_out)[target].reshape(peer_count, per_peer, row_width)
            )
            returned_logs.append(
                with_zero_row(logs_out)[target].reshape(peer_count, per_peer, local_heads)
            )
        back_rows, back_logs = (
            lax.all_to_all(
                jnp.stack(returned_rows, axis=1).astype(jnp.float32),
                "ctx",
                split_axis=0,
                concat_axis=0,
                tiled=True,
            ).astype(jnp.bfloat16),
            lax.all_to_all(
                jnp.stack(returned_logs, axis=1), "ctx", split_axis=0, concat_axis=0, tiled=True
            ),
        )
        for member_index, round_index in enumerate(round_group):
            round_outputs[round_index] = homeward(back_rows[:, member_index], round_index)
            round_logs[round_index] = homeward(back_logs[:, member_index], round_index)
    log_stack = jnp.stack(round_logs)
    largest = jnp.max(log_stack, axis=0)
    lifted = jnp.exp(log_stack - largest)
    round_weight = lifted / jnp.sum(lifted, axis=0)
    row_stack = (
        jnp.stack(round_outputs)
        .astype(jnp.float32)
        .reshape(rounds, token_rows, local_heads, HEAD_DIM)
    )
    attended = (
        jnp.sum(round_weight[..., None] * row_stack, axis=0)
        .reshape(token_rows, row_width)
        .astype(jnp.bfloat16)
    )
    partial_value = lax.dot_general(
        attended, whole_weight, (((1,), (1,)), ((), ())), preferred_element_type=jnp.float32
    )
    mixed = lax.psum_scatter(partial_value, "head", scatter_dimension=1, tiled=True).astype(
        jnp.bfloat16
    )
    full_grad = lax.all_gather(out_grad, "head", axis=1, tiled=True)
    attended_grad = jnp.dot(full_grad, whole_weight, preferred_element_type=jnp.float32)
    token_total = token_rows * peer_count
    grad_weight = lax.psum_scatter(
        lax.dot_general(
            full_grad, attended, (((0,), (0,)), ((), ())), preferred_element_type=jnp.float32
        ),
        "ctx",
        scatter_dimension=0,
        tiled=True,
    ) * (1.0 / math.sqrt(token_total))
    grad_heads = attended_grad.reshape(token_rows, local_heads, HEAD_DIM)
    inner = jnp.sum(
        grad_heads * attended.astype(jnp.float32).reshape(token_rows, local_heads, HEAD_DIM),
        axis=-1,
    )
    qk_total = jnp.zeros((token_rows, row_width), jnp.float32)
    value_total = jnp.zeros((token_rows, row_width), jnp.float32)
    for round_group in groups:
        send_grad = jnp.stack(
            [
                outgoing(
                    with_zero_row(
                        (round_weight[round_index][..., None] * grad_heads)
                        .reshape(token_rows, row_width)
                        .astype(jnp.bfloat16)
                    ),
                    round_index,
                )
                for round_index in round_group
            ],
            axis=1,
        )
        send_shift = jnp.stack(
            [
                outgoing(with_zero_row(round_weight[round_index] * inner), round_index)
                for round_index in round_group
            ],
            axis=1,
        )
        got_grad, got_shift = (
            lax.all_to_all(
                send_grad.astype(jnp.float32), "ctx", split_axis=0, concat_axis=0, tiled=True
            ).astype(send_grad.dtype),
            lax.all_to_all(send_shift, "ctx", split_axis=0, concat_axis=0, tiled=True),
        )
        returned_qk = []
        returned_values = []
        for member_index, round_index in enumerate(round_group):
            own_qk, own_values, occupied, source_slot, target = owner_state[round_index]
            own_grad = with_zero_row(got_grad[:, member_index].reshape(capacity, row_width))[
                source_slot
            ]
            own_shift = with_zero_row(got_shift[:, member_index].reshape(capacity, local_heads))[
                source_slot
            ]
            qk_rows, value_rows = owner_backward(
                own_qk, own_values, occupied, own_grad, own_shift, local_heads
            )
            returned_qk.append(
                with_zero_row(qk_rows)[target].reshape(peer_count, per_peer, row_width)
            )
            returned_values.append(
                with_zero_row(value_rows)[target].reshape(peer_count, per_peer, row_width)
            )
        back_qk, back_values = (
            lax.all_to_all(
                jnp.stack(returned_qk, axis=1), "ctx", split_axis=0, concat_axis=0, tiled=True
            ),
            lax.all_to_all(
                jnp.stack(returned_values, axis=1), "ctx", split_axis=0, concat_axis=0, tiled=True
            ),
        )
        for member_index, round_index in enumerate(round_group):
            qk_total = qk_total + homeward(back_qk[:, member_index], round_index).astype(
                jnp.float32
            )
            value_total = value_total + homeward(back_values[:, member_index], round_index).astype(
                jnp.float32
            )
    return (mixed, qk_total.astype(jnp.bfloat16), value_total.astype(jnp.bfloat16), grad_weight)


PLANES = 4
TALL = 256
HALF = 64
VMEM_BYTES = 48 * 1024 * 1024


def contract(left, right, left_dim, right_dim):
    return lax.dot_general(
        left, right, (((left_dim,), (right_dim,)), ((), ())), preferred_element_type=jnp.float32
    )


def slot_pick(slot_ref, source):
    slot_ids = lax.broadcasted_iota(jnp.int32, (TALL, SPAN), 0)
    return (slot_ids == slot_ref[pl.ds(source, 1), :]).astype(jnp.bfloat16)


def bucket_scores(rows, code_ref, bucket):
    scores = contract(rows, rows, 1, 1) * HEAD_DIM ** (-0.5)
    key_ids = lax.broadcasted_iota(jnp.int32, (TALL, TALL), 0)
    query_ids = lax.broadcasted_iota(jnp.int32, (TALL, TALL), 1)
    scores = jnp.where(key_ids == query_ids, scores - self_penalty, scores)
    code_row = code_ref[pl.ds(bucket, 1), :]
    code_column = jnp.broadcast_to(code_row, (SPAN, TALL)).T
    code_column = jnp.concatenate([code_column, code_column], axis=1)
    seen = (code_column > 0.5) & (code_column <= jnp.maximum(code_row, 1.0))
    return jnp.where(seen, scores, masked_score)


def forward_kernel(mine_ref, other_ref, slot_ref, code_ref, out_ref, log_ref, grouped, results):
    sources, slots = grouped.shape[0], grouped.shape[1]
    per_peer = TALL // sources
    buckets = slots // per_peer

    def group(source, carry):
        rows = jnp.concatenate([mine_ref[source, :HALF], other_ref[source]], axis=0)
        grouped[source] = contract(slot_pick(slot_ref, source), rows, 1, 0)
        return carry

    lax.fori_loop(0, sources, group, 0, unroll=2)

    def attend(bucket, carry):
        place = pl.ds(pl.multiple_of(bucket * per_peer, per_peer), per_peer)
        rows = grouped[:, place, :].reshape(TALL, 2 * HEAD_DIM).astype(jnp.bfloat16)
        scores = bucket_scores(rows[:, :HEAD_DIM], code_ref, bucket)
        largest = jnp.max(scores, axis=0, keepdims=True)
        lifted = jnp.exp(scores - largest)
        summed = jnp.sum(lifted, axis=0, keepdims=True)
        probability = (lifted / summed).astype(jnp.bfloat16)
        result = contract(probability, rows[:, HEAD_DIM:], 0, 0)
        results[:, place, :] = result.reshape(sources, per_peer, HEAD_DIM)
        log_ref[pl.ds(bucket, 1), :] = largest + jnp.log(summed)
        return carry

    lax.fori_loop(0, buckets, attend, 0, unroll=2)

    def scatter(source, carry):
        rows = results[source].astype(jnp.bfloat16)
        out_ref[source] = contract(slot_pick(slot_ref, source), rows, 0, 0).astype(jnp.bfloat16)
        return carry

    lax.fori_loop(0, sources, scatter, 0, unroll=2)


def backward_kernel(
    mine_ref, other_ref, grad_ref, slot_ref, code_ref, log_ref, shift_ref, out_ref, grouped, results
):
    sources, slots = grouped.shape[0], grouped.shape[1]
    per_peer = TALL // sources
    buckets = slots // per_peer
    both = 2 * HEAD_DIM

    def group(source, carry):
        rows = jnp.concatenate([mine_ref[source, :HALF], other_ref[source]], axis=0)
        pick = slot_pick(slot_ref, source)
        grouped[source, :, :both] = contract(pick, rows, 1, 0)
        grouped[source, :, both:] = contract(pick, grad_ref[source], 1, 0)
        return carry

    lax.fori_loop(0, sources, group, 0, unroll=2)

    def attend(bucket, carry):
        place = pl.ds(pl.multiple_of(bucket * per_peer, per_peer), per_peer)
        rows = grouped[:, place, :].reshape(TALL, 3 * HEAD_DIM).astype(jnp.bfloat16)
        qk_rows, value_rows, grad_rows = (
            rows[:, :HEAD_DIM],
            rows[:, HEAD_DIM:both],
            rows[:, both:],
        )
        scores = bucket_scores(qk_rows, code_ref, bucket)
        probability = jnp.exp(scores - log_ref[pl.ds(bucket, 1), :])
        prob_grad = contract(value_rows, grad_rows, 1, 1)
        score_grad = (probability * (prob_grad - shift_ref[pl.ds(bucket, 1), :])).astype(
            jnp.bfloat16
        )
        qk_grad = contract(score_grad, qk_rows, 0, 0) + contract(score_grad, qk_rows, 1, 0)
        value_grad = contract(probability.astype(jnp.bfloat16), grad_rows, 1, 0)
        results[:, place, :HEAD_DIM] = (qk_grad * HEAD_DIM ** (-0.5)).reshape(
            sources, per_peer, HEAD_DIM
        )
        results[:, place, HEAD_DIM:] = value_grad.reshape(sources, per_peer, HEAD_DIM)
        return carry

    lax.fori_loop(0, buckets, attend, 0, unroll=2)

    def scatter(source, carry):
        rows = results[source].astype(jnp.bfloat16)
        out_ref[source] = contract(slot_pick(slot_ref, source), rows, 0, 0).astype(jnp.bfloat16)
        return carry

    lax.fori_loop(0, sources, scatter, 0, unroll=2)


def kernel_call(body, out_shape, scratch_shapes, arguments):
    return pl.pallas_call(
        body,
        out_shape=out_shape,
        in_specs=[pl.BlockSpec(memory_space=pltpu.VMEM)] * len(arguments),
        out_specs=jax.tree.map(lambda _: pl.BlockSpec(memory_space=pltpu.VMEM), out_shape),
        scratch_shapes=scratch_shapes,
        compiler_params=pltpu.CompilerParams(vmem_limit_bytes=VMEM_BYTES),
    )(*arguments)


def head_owner_device(shared_qk, values, out_grad, out_weight, buckets):
    token_rows, row_width = shared_qk.shape
    heads = row_width // HEAD_DIM
    peers = lax.axis_size("ctx")
    per_peer = 2 * token_rows // peers
    half = token_rows // 2
    slots = peers * per_peer
    core = lax.axis_index("ctx") % 2
    first = core == 0
    partners = [(device, device ^ 1) for device in range(peers)]

    def exchange(block):
        return lax.ppermute(block, "ctx", partners)

    def swapped(block):
        return jnp.concatenate([block[:, half:], block[:, :half]], axis=1)

    def everywhere(block):
        return lax.all_to_all(block, "ctx", split_axis=0, concat_axis=0, tiled=True)

    def by_head(rows):
        return rows.reshape(2, half, heads, HEAD_DIM).transpose(2, 0, 1, 3)

    def by_token(blocks):
        return blocks.reshape(heads, 2, half, HEAD_DIM).transpose(1, 2, 0, 3).reshape(
            token_rows, row_width
        )

    def own_half(rows):
        parted = rows.reshape(rows.shape[0], heads, 2, -1)
        even, odd = parted[:, :, 0], parted[:, :, 1]
        kept, passed = jnp.where(first, even, odd), jnp.where(first, odd, even)
        return kept.reshape(rows.shape[0], -1), passed.reshape(rows.shape[0], -1)

    plane = peers // PLANES
    index = lax.axis_index("ctx")
    level, here, seat = index // plane, index % plane, index % PLANES
    up = [
        [
            (PLANES * place + (tier - step) % PLANES, tier * plane + place)
            for tier in range(PLANES)
            for place in range(plane)
        ]
        for step in range(PLANES)
    ]

    def pick(blocks, which):
        return lax.dynamic_index_in_dim(blocks, which, axis=0, keepdims=False)

    def moved(block, mask):
        return lax.ppermute(block, "ctx", [(device, device ^ mask) for device in range(peers)])

    half_weight = lax.all_gather(
        out_weight,
        "ctx",
        axis=0,
        tiled=True,
        axis_index_groups=[list(range(0, peers, 2)), list(range(1, peers, 2))],
    )

    tag = jnp.pad(buckets.astype(jnp.bfloat16).reshape(1, -1), ((0, 7), (0, 0)))
    sent = jnp.concatenate([by_head(shared_qk), by_head(values)], axis=-1)
    sent = jnp.concatenate(
        [
            sent.reshape(peers, half, 2 * HEAD_DIM),
            jnp.broadcast_to(tag[None], (peers, 8, 2 * HEAD_DIM)),
        ],
        axis=1,
    )
    mine = everywhere(sent)
    left, right = out_grad[:, : row_width // 2], out_grad[:, row_width // 2 :]
    left_two = jnp.concatenate([left, moved(left, 2)], axis=0)
    right_x = moved(right, 4)
    right_two = jnp.concatenate([right, right_x], axis=0)
    left_four = jnp.concatenate([left_two, moved(left_two, 4)], axis=0)
    right_far = moved(right_two, 2)
    right_four = jnp.concatenate(
        [right, right_far[:token_rows], right_x, right_far[token_rows:]], axis=0
    )
    core_grad = jnp.concatenate([left_four, right_four], axis=1)
    plane_grad = jnp.concatenate([core_grad, exchange(core_grad)], axis=0)
    mine, plane_grad = lax.optimization_barrier((mine, plane_grad))
    other = exchange(mine[:, :half])

    all_buckets = mine[:, half].astype(jnp.int32).reshape(peers, 2, token_rows)
    own = jnp.where(first, all_buckets[:, 0], all_buckets[:, 1])
    order = jnp.arange(token_rows, dtype=jnp.int32)
    same = (own[:, :, None] == own[:, None, :]) & (order[None, :] < order[:, None])[None]
    position = jnp.sum(same.astype(jnp.int32), axis=2)
    slot = own * per_peer + position
    slot = jnp.where(first, slot, swapped(slot))
    bucket_ids = jnp.arange(peers, dtype=jnp.int32)
    counts = jnp.sum((own[:, :, None] == bucket_ids).astype(jnp.int32), axis=1)
    before = (bucket_ids[None, :] < bucket_ids[:, None]).astype(jnp.int32)
    starts = jnp.sum(before[:, :, None] * counts[None], axis=1)
    within = jnp.arange(per_peer, dtype=jnp.int32)
    live = within < counts[:, :, None]
    code = jnp.where(live, jnp.where(starts[:, :, None] + within >= SPAN, 2.0, 1.0), 0.0)
    code = code.astype(jnp.float32).transpose(1, 0, 2).reshape(peers, peers * per_peer)

    result, log_slots = kernel_call(
        forward_kernel,
        (
            jax.ShapeDtypeStruct((peers, token_rows, HEAD_DIM), jnp.bfloat16),
            jax.ShapeDtypeStruct((peers, peers * per_peer), jnp.float32),
        ),
        [
            pltpu.VMEM((peers, slots, 2 * HEAD_DIM), jnp.float32),
            pltpu.VMEM((peers, slots, HEAD_DIM), jnp.float32),
        ],
        (mine, other, slot, code),
    )

    chosen = slot[:, :, None] == jnp.arange(slots, dtype=jnp.int32)
    log_by_source = log_slots.reshape(peers, peers, per_peer).transpose(1, 0, 2).reshape(peers, slots)
    log_own = jnp.sum(jnp.where(chosen, log_by_source[:, None, :], 0.0), axis=2)
    log_other = swapped(exchange(log_own))
    result_other = swapped(exchange(result))
    largest = jnp.maximum(log_own, log_other)
    lifted_own, lifted_other = jnp.exp(log_own - largest), jnp.exp(log_other - largest)
    lifted_sum = lifted_own + lifted_other
    weight_own, weight_other = lifted_own / lifted_sum, lifted_other / lifted_sum
    attended = (
        weight_own[:, :, None] * result.astype(jnp.float32)
        + weight_other[:, :, None] * result_other.astype(jnp.float32)
    ).astype(jnp.bfloat16)

    grad_kept, grad_passed = own_half(out_grad)
    grad_pair = jnp.concatenate([grad_kept, exchange(grad_passed)], axis=0)
    grad_pair, attended = lax.optimization_barrier((grad_pair, attended))
    attended_rows = by_token(everywhere(attended[:, :half]))
    grad_part = jnp.dot(grad_pair, half_weight, preferred_element_type=jnp.float32)
    attended_grad = (grad_part[:token_rows] + exchange(grad_part[token_rows:])).astype(
        jnp.bfloat16
    )
    attended_grad, attended_rows = lax.optimization_barrier((attended_grad, attended_rows))
    grad_mine = everywhere(by_head(attended_grad).reshape(peers, half, HEAD_DIM))
    grad_rows = jnp.concatenate([grad_mine, exchange(grad_mine)], axis=1).astype(jnp.float32)

    inner = jnp.sum(grad_rows * attended.astype(jnp.float32), axis=-1)
    shift = weight_own * inner
    query_grad = (weight_own[:, :, None] * grad_rows).astype(jnp.bfloat16)
    shift_slots = jnp.sum(jnp.where(chosen, shift[:, :, None], 0.0), axis=1)
    shift_slots = (
        shift_slots.reshape(peers, peers, per_peer).transpose(1, 0, 2).reshape(peers, slots)
    )

    attended_pair = jnp.concatenate([attended_rows, exchange(attended_rows)], axis=0)
    mixed_part = contract(attended_pair, half_weight, 1, 1).astype(jnp.bfloat16)
    mixed_kept, mixed_got = mixed_part[:token_rows], exchange(mixed_part[token_rows:])
    mixed_even = jnp.where(first, mixed_kept, mixed_got).reshape(token_rows, heads, 1, -1)
    mixed_odd = jnp.where(first, mixed_got, mixed_kept).reshape(token_rows, heads, 1, -1)
    mixed = jnp.concatenate([mixed_even, mixed_odd], axis=2).reshape(token_rows, row_width)

    attended_half = attended[:, :half].reshape(PLANES, plane * half, HEAD_DIM)
    arrived = jnp.stack(
        [
            lax.ppermute(pick(attended_half, (seat + step) % PLANES), "ctx", up[step])
            for step in range(PLANES)
        ]
    )
    plane_attended = (
        jnp.stack([pick(arrived, (level - place) % PLANES) for place in range(PLANES)])
        .reshape(2, 2, plane, half, HEAD_DIM)
        .transpose(2, 1, 3, 0, 4)
        .reshape(plane, token_rows, row_width // plane)
    )
    plane_attended = jnp.concatenate(
        [pick(plane_attended, here ^ mask) for mask in (0, 2, 4, 6, 1, 3, 5, 7)], axis=0
    )
    partial = contract(plane_grad, plane_attended, 0, 0) * (1.0 / math.sqrt(token_rows * peers))
    partial = partial.astype(jnp.bfloat16).reshape(
        peers, row_width // peers, row_width // plane
    )
    query_grad, partial = lax.optimization_barrier((query_grad, partial))
    shares = everywhere(partial)
    shares = shares.reshape((PLANES, plane) + shares.shape[1:]).astype(jnp.float32)
    grad_weight = jnp.sum(shares, axis=0).transpose(1, 0, 2).reshape(-1, row_width)

    grads = kernel_call(
        backward_kernel,
        jax.ShapeDtypeStruct((peers, token_rows, 2 * HEAD_DIM), jnp.bfloat16),
        [
            pltpu.VMEM((peers, slots, 3 * HEAD_DIM), jnp.float32),
            pltpu.VMEM((peers, slots, 2 * HEAD_DIM), jnp.float32),
        ],
        (mine, other, query_grad, slot, code, log_slots, shift_slots),
    )
    grads_other = exchange(grads[:, half:])
    total = (grads[:, :half].astype(jnp.float32) + grads_other.astype(jnp.float32)).astype(
        jnp.bfloat16
    )
    back = everywhere(total)
    grad_qk = by_token(back[:, :, :HEAD_DIM])
    grad_values = by_token(back[:, :, HEAD_DIM:])

    return (mixed, grad_qk, grad_values, grad_weight)


def per_device(shared_qk, values, out_grad, out_weight, buckets):
    token_rows, row_width = shared_qk.shape
    peers = lax.axis_size("ctx")
    fits = (
        lax.axis_size("head") == 1
        and buckets.shape[0] == 2
        and peers == 2 * (row_width // HEAD_DIM)
        and 2 * token_rows == TALL
        and TALL // peers == 8
    )
    whole = head_owner_device if fits else bucket_owner_device
    return whole(shared_qk, values, out_grad, out_weight, buckets)


def solution(mesh):
    in_specs = (
        P("ctx", "head"),
        P("ctx", "head"),
        P("ctx", "head"),
        P("ctx", "head"),
        P(None, "ctx"),
    )
    out_specs = (P("ctx", "head"), P("ctx", "head"), P("ctx", "head"), P("ctx", "head"))
    return jax.shard_map(
        per_device, mesh=mesh, in_specs=in_specs, out_specs=out_specs, check_vma=False
    )
```

```python
import math

import jax
import jax.numpy as jnp
from jax import lax
from jax.experimental import pallas as pl
from jax.experimental.pallas import tpu as pltpu
from jax.sharding import PartitionSpec as P

HEAD_DIM = 128
SPAN = 128


self_penalty = 10000.0
masked_score = -1e30


def with_zero_row(matrix):
    return jnp.concatenate([matrix, jnp.zeros((1,) + matrix.shape[1:], matrix.dtype)], axis=0)


def key_windows(rows):
    row_count = rows.shape[0]
    leading = jnp.zeros((SPAN,) + rows.shape[1:], rows.dtype)
    earlier = jnp.concatenate([leading, rows[: row_count - SPAN]], axis=0)
    shape_out = (row_count // SPAN, SPAN) + rows.shape[1:]
    return jnp.concatenate([earlier.reshape(shape_out), rows.reshape(shape_out)], axis=1)


def fold_windows(stacked):
    current = stacked[:, SPAN:]
    earlier = stacked[:, :SPAN]
    return current + jnp.concatenate([earlier[1:], jnp.zeros_like(earlier[:1])], axis=0)


def span_probs(queries, key_rows, key_live):
    scores = jnp.einsum(
        "qhd,khd->hqk", queries, key_rows, preferred_element_type=jnp.float32
    ) * HEAD_DIM ** (-0.5)
    itself = jnp.arange(2 * SPAN)[None, :] == jnp.arange(SPAN)[:, None] + SPAN
    scores = jnp.where(itself[None], scores - self_penalty, scores)
    scores = jnp.where(key_live[None, None, :], scores, masked_score)
    largest = jnp.max(scores, axis=-1, keepdims=True)
    lifted = jnp.exp(scores - largest)
    summed = jnp.sum(lifted, axis=-1, keepdims=True)
    return (lifted / summed, (largest + jnp.log(summed))[..., 0])


def owner_forward(own_qk, own_values, occupied, local_heads):
    blocks = own_qk.shape[0] // SPAN
    queries = own_qk.reshape(blocks, SPAN, local_heads, HEAD_DIM)
    key_rows = key_windows(own_qk).reshape(blocks, 2 * SPAN, local_heads, HEAD_DIM)
    value_rows = key_windows(own_values).reshape(blocks, 2 * SPAN, local_heads, HEAD_DIM)
    live_keys = key_windows(occupied)

    def one_block(pieces):
        block_query, block_key, block_value, block_live = pieces
        probability, log_total = span_probs(block_query, block_key, block_live)
        result = jnp.einsum(
            "hqk,khd->qhd",
            probability.astype(jnp.bfloat16),
            block_value,
            preferred_element_type=jnp.float32,
        )
        return (result.astype(jnp.bfloat16).reshape(SPAN, local_heads * HEAD_DIM), log_total.T)

    outputs, log_totals = lax.map(one_block, (queries, key_rows, value_rows, live_keys))
    return (outputs.reshape(-1, local_heads * HEAD_DIM), log_totals.reshape(-1, local_heads))


def owner_backward(own_qk, own_values, occupied, own_grad, own_shift, local_heads):
    blocks = own_qk.shape[0] // SPAN
    queries = own_qk.reshape(blocks, SPAN, local_heads, HEAD_DIM)
    key_rows = key_windows(own_qk).reshape(blocks, 2 * SPAN, local_heads, HEAD_DIM)
    value_rows = key_windows(own_values).reshape(blocks, 2 * SPAN, local_heads, HEAD_DIM)
    live_keys = key_windows(occupied)
    grad_rows = own_grad.reshape(blocks, SPAN, local_heads, HEAD_DIM)
    shift_rows = own_shift.reshape(blocks, SPAN, local_heads)

    def one_block(pieces):
        block_query, block_key, block_value, block_live, block_grad, block_shift = pieces
        probability, log_total = span_probs(block_query, block_key, block_live)
        prob_grad = jnp.einsum(
            "qhd,khd->hqk", block_grad, block_value, preferred_element_type=jnp.float32
        )
        score_grad = (probability * (prob_grad - block_shift.T[:, :, None])).astype(jnp.bfloat16)
        query_grad = jnp.einsum(
            "hqk,khd->qhd", score_grad, block_key, preferred_element_type=jnp.float32
        ) * HEAD_DIM ** (-0.5)
        key_grad = jnp.einsum(
            "hqk,qhd->khd", score_grad, block_query, preferred_element_type=jnp.float32
        ) * HEAD_DIM ** (-0.5)
        value_grad = jnp.einsum(
            "hqk,qhd->khd",
            probability.astype(jnp.bfloat16),
            block_grad,
            preferred_element_type=jnp.float32,
        )
        return (query_grad, key_grad, value_grad)

    query_grad, key_grad, value_grad = lax.map(
        one_block, (queries, key_rows, value_rows, live_keys, grad_rows, shift_rows)
    )
    row_width = local_heads * HEAD_DIM
    qk_rows = (query_grad + fold_windows(key_grad)).reshape(-1, row_width).astype(jnp.bfloat16)
    value_out = fold_windows(value_grad).reshape(-1, row_width).astype(jnp.bfloat16)
    return (qk_rows, value_out)


def route_round(bucket_row, peer_count, per_peer, token_rows):
    owners = jnp.arange(peer_count, dtype=jnp.int32)
    member = (bucket_row[:, None] == owners[None, :]).astype(jnp.int32)
    earlier = jnp.cumsum(member, axis=0) - member
    position = jnp.sum(earlier * member, axis=1)
    slot_index = bucket_row * per_peer + position
    slot_token = (
        jnp.full((peer_count * per_peer,), token_rows, jnp.int32)
        .at[slot_index]
        .set(jnp.arange(token_rows, dtype=jnp.int32))
    )
    return (slot_index, slot_token)


def compact_slots(slot_marks, capacity):
    target = jnp.cumsum(slot_marks) - 1
    target = jnp.where(slot_marks > 0, target, capacity).astype(jnp.int32)
    source_slot = (
        jnp.full((capacity,), capacity, jnp.int32)
        .at[target]
        .set(jnp.arange(capacity, dtype=jnp.int32), mode="drop")
    )
    return (source_slot, target)


def bucket_owner_device(shared_qk, values, out_grad, out_weight, buckets):
    token_rows, row_width = shared_qk.shape
    local_heads = row_width // HEAD_DIM
    peer_count = lax.axis_size("ctx")
    capacity = 2 * token_rows
    per_peer = capacity // peer_count
    rounds = buckets.shape[0]
    routes = [
        route_round(buckets[round_index], peer_count, per_peer, token_rows)
        for round_index in range(rounds)
    ]
    padded_qk = with_zero_row(shared_qk)
    padded_values = with_zero_row(values)
    whole_weight = lax.all_gather(out_weight, "ctx", axis=0, tiled=True)
    groups = [[round_index] for round_index in range(rounds)]

    def outgoing(matrix, round_index):
        return matrix[routes[round_index][1]].reshape((peer_count, per_peer) + matrix.shape[1:])

    def homeward(received, round_index):
        flat_rows = received.reshape((peer_count * per_peer,) + received.shape[2:])
        return flat_rows[routes[round_index][0]]

    round_outputs = [None] * rounds
    round_logs = [None] * rounds
    owner_state = [None] * rounds
    for round_group in groups:
        send_qk = jnp.stack(
            [outgoing(padded_qk, round_index) for round_index in round_group], axis=1
        )
        send_values = jnp.stack(
            [outgoing(padded_values, round_index) for round_index in round_group], axis=1
        )
        slot_marks = jnp.stack(
            [
                (routes[round_index][1] < token_rows)
                .astype(jnp.int32)
                .reshape(peer_count, per_peer)
                for round_index in round_group
            ],
            axis=1,
        )
        got_qk, got_values, got_marks = (
            lax.all_to_all(send_qk, "ctx", split_axis=0, concat_axis=0, tiled=True),
            lax.all_to_all(send_values, "ctx", split_axis=0, concat_axis=0, tiled=True),
            lax.all_to_all(slot_marks, "ctx", split_axis=0, concat_axis=0, tiled=True),
        )
        returned_rows = []
        returned_logs = []
        for member_index, round_index in enumerate(round_group):
            source_slot, target = compact_slots(got_marks[:, member_index].reshape(-1), capacity)
            own_qk = with_zero_row(got_qk[:, member_index].reshape(capacity, row_width))[
                source_slot
            ]
            own_values = with_zero_row(got_values[:, member_index].reshape(capacity, row_width))[
                source_slot
            ]
            occupied = source_slot < capacity
            rows_out, logs_out = owner_forward(own_qk, own_values, occupied, local_heads)
            owner_state[round_index] = (own_qk, own_values, occupied, source_slot, target)
            returned_rows.append(
                with_zero_row(rows_out)[target].reshape(peer_count, per_peer, row_width)
            )
            returned_logs.append(
                with_zero_row(logs_out)[target].reshape(peer_count, per_peer, local_heads)
            )
        back_rows, back_logs = (
            lax.all_to_all(
                jnp.stack(returned_rows, axis=1).astype(jnp.float32),
                "ctx",
                split_axis=0,
                concat_axis=0,
                tiled=True,
            ).astype(jnp.bfloat16),
            lax.all_to_all(
                jnp.stack(returned_logs, axis=1), "ctx", split_axis=0, concat_axis=0, tiled=True
            ),
        )
        for member_index, round_index in enumerate(round_group):
            round_outputs[round_index] = homeward(back_rows[:, member_index], round_index)
            round_logs[round_index] = homeward(back_logs[:, member_index], round_index)
    log_stack = jnp.stack(round_logs)
    largest = jnp.max(log_stack, axis=0)
    lifted = jnp.exp(log_stack - largest)
    round_weight = lifted / jnp.sum(lifted, axis=0)
    row_stack = (
        jnp.stack(round_outputs)
        .astype(jnp.float32)
        .reshape(rounds, token_rows, local_heads, HEAD_DIM)
    )
    attended = (
        jnp.sum(round_weight[..., None] * row_stack, axis=0)
        .reshape(token_rows, row_width)
        .astype(jnp.bfloat16)
    )
    partial_value = lax.dot_general(
        attended, whole_weight, (((1,), (1,)), ((), ())), preferred_element_type=jnp.float32
    )
    mixed = lax.psum_scatter(partial_value, "head", scatter_dimension=1, tiled=True).astype(
        jnp.bfloat16
    )
    full_grad = lax.all_gather(out_grad, "head", axis=1, tiled=True)
    attended_grad = jnp.dot(full_grad, whole_weight, preferred_element_type=jnp.float32)
    token_total = token_rows * peer_count
    grad_weight = lax.psum_scatter(
        lax.dot_general(
            full_grad, attended, (((0,), (0,)), ((), ())), preferred_element_type=jnp.float32
        ),
        "ctx",
        scatter_dimension=0,
        tiled=True,
    ) * (1.0 / math.sqrt(token_total))
    grad_heads = attended_grad.reshape(token_rows, local_heads, HEAD_DIM)
    inner = jnp.sum(
        grad_heads * attended.astype(jnp.float32).reshape(token_rows, local_heads, HEAD_DIM),
        axis=-1,
    )
    qk_total = jnp.zeros((token_rows, row_width), jnp.float32)
    value_total = jnp.zeros((token_rows, row_width), jnp.float32)
    for round_group in groups:
        send_grad = jnp.stack(
            [
                outgoing(
                    with_zero_row(
                        (round_weight[round_index][..., None] * grad_heads)
                        .reshape(token_rows, row_width)
                        .astype(jnp.bfloat16)
                    ),
                    round_index,
                )
                for round_index in round_group
            ],
            axis=1,
        )
        send_shift = jnp.stack(
            [
                outgoing(with_zero_row(round_weight[round_index] * inner), round_index)
                for round_index in round_group
            ],
            axis=1,
        )
        got_grad, got_shift = (
            lax.all_to_all(
                send_grad.astype(jnp.float32), "ctx", split_axis=0, concat_axis=0, tiled=True
            ).astype(send_grad.dtype),
            lax.all_to_all(send_shift, "ctx", split_axis=0, concat_axis=0, tiled=True),
        )
        returned_qk = []
        returned_values = []
        for member_index, round_index in enumerate(round_group):
            own_qk, own_values, occupied, source_slot, target = owner_state[round_index]
            own_grad = with_zero_row(got_grad[:, member_index].reshape(capacity, row_width))[
                source_slot
            ]
            own_shift = with_zero_row(got_shift[:, member_index].reshape(capacity, local_heads))[
                source_slot
            ]
            qk_rows, value_rows = owner_backward(
                own_qk, own_values, occupied, own_grad, own_shift, local_heads
            )
            returned_qk.append(
                with_zero_row(qk_rows)[target].reshape(peer_count, per_peer, row_width)
            )
            returned_values.append(
                with_zero_row(value_rows)[target].reshape(peer_count, per_peer, row_width)
            )
        back_qk, back_values = (
            lax.all_to_all(
                jnp.stack(returned_qk, axis=1), "ctx", split_axis=0, concat_axis=0, tiled=True
            ),
            lax.all_to_all(
                jnp.stack(returned_values, axis=1), "ctx", split_axis=0, concat_axis=0, tiled=True
            ),
        )
        for member_index, round_index in enumerate(round_group):
            qk_total = qk_total + homeward(back_qk[:, member_index], round_index).astype(
                jnp.float32
            )
            value_total = value_total + homeward(back_values[:, member_index], round_index).astype(
                jnp.float32
            )
    return (mixed, qk_total.astype(jnp.bfloat16), value_total.astype(jnp.bfloat16), grad_weight)


PLANES = 4
TALL = 256
HALF = 64
VMEM_BYTES = 48 * 1024 * 1024


def contract(left, right, left_dim, right_dim):
    return lax.dot_general(
        left, right, (((left_dim,), (right_dim,)), ((), ())), preferred_element_type=jnp.float32
    )


def slot_pick(slot_ref, source):
    slot_ids = lax.broadcasted_iota(jnp.int32, (TALL, SPAN), 0)
    return (slot_ids == slot_ref[pl.ds(source, 1), :]).astype(jnp.bfloat16)


def bucket_scores(rows, code_ref, bucket):
    scores = contract(rows, rows, 1, 1) * HEAD_DIM ** (-0.5)
    key_ids = lax.broadcasted_iota(jnp.int32, (TALL, TALL), 0)
    query_ids = lax.broadcasted_iota(jnp.int32, (TALL, TALL), 1)
    scores = jnp.where(key_ids == query_ids, scores - self_penalty, scores)
    code_row = code_ref[pl.ds(bucket, 1), :]
    code_column = jnp.broadcast_to(code_row, (SPAN, TALL)).T
    code_column = jnp.concatenate([code_column, code_column], axis=1)
    seen = (code_column > 0.5) & (code_column <= jnp.maximum(code_row, 1.0))
    return jnp.where(seen, scores, masked_score)


def forward_kernel(mine_ref, other_ref, slot_ref, code_ref, out_ref, log_ref, grouped, results):
    sources, slots = grouped.shape[0], grouped.shape[1]
    per_peer = TALL // sources
    buckets = slots // per_peer

    def group(source, carry):
        rows = jnp.concatenate([mine_ref[source, :HALF], other_ref[source]], axis=0)
        grouped[source] = contract(slot_pick(slot_ref, source), rows, 1, 0)
        return carry

    lax.fori_loop(0, sources, group, 0, unroll=2)

    def attend(bucket, carry):
        place = pl.ds(pl.multiple_of(bucket * per_peer, per_peer), per_peer)
        rows = grouped[:, place, :].reshape(TALL, 2 * HEAD_DIM).astype(jnp.bfloat16)
        scores = bucket_scores(rows[:, :HEAD_DIM], code_ref, bucket)
        largest = jnp.max(scores, axis=0, keepdims=True)
        lifted = jnp.exp(scores - largest)
        summed = jnp.sum(lifted, axis=0, keepdims=True)
        probability = (lifted / summed).astype(jnp.bfloat16)
        result = contract(probability, rows[:, HEAD_DIM:], 0, 0)
        results[:, place, :] = result.reshape(sources, per_peer, HEAD_DIM)
        log_ref[pl.ds(bucket, 1), :] = largest + jnp.log(summed)
        return carry

    lax.fori_loop(0, buckets, attend, 0, unroll=2)

    def scatter(source, carry):
        rows = results[source].astype(jnp.bfloat16)
        out_ref[source] = contract(slot_pick(slot_ref, source), rows, 0, 0).astype(jnp.bfloat16)
        return carry

    lax.fori_loop(0, sources, scatter, 0, unroll=2)


def backward_kernel(
    mine_ref, other_ref, grad_ref, slot_ref, code_ref, log_ref, shift_ref, out_ref, grouped, results
):
    sources, slots = grouped.shape[0], grouped.shape[1]
    per_peer = TALL // sources
    buckets = slots // per_peer
    both = 2 * HEAD_DIM

    def group(source, carry):
        rows = jnp.concatenate([mine_ref[source, :HALF], other_ref[source]], axis=0)
        pick = slot_pick(slot_ref, source)
        grouped[source, :, :both] = contract(pick, rows, 1, 0)
        grouped[source, :, both:] = contract(pick, grad_ref[source], 1, 0)
        return carry

    lax.fori_loop(0, sources, group, 0, unroll=2)

    def attend(bucket, carry):
        place = pl.ds(pl.multiple_of(bucket * per_peer, per_peer), per_peer)
        rows = grouped[:, place, :].reshape(TALL, 3 * HEAD_DIM).astype(jnp.bfloat16)
        qk_rows, value_rows, grad_rows = (
            rows[:, :HEAD_DIM],
            rows[:, HEAD_DIM:both],
            rows[:, both:],
        )
        scores = bucket_scores(qk_rows, code_ref, bucket)
        probability = jnp.exp(scores - log_ref[pl.ds(bucket, 1), :])
        prob_grad = contract(value_rows, grad_rows, 1, 1)
        score_grad = (probability * (prob_grad - shift_ref[pl.ds(bucket, 1), :])).astype(
            jnp.bfloat16
        )
        qk_grad = contract(score_grad, qk_rows, 0, 0) + contract(score_grad, qk_rows, 1, 0)
        value_grad = contract(probability.astype(jnp.bfloat16), grad_rows, 1, 0)
        results[:, place, :HEAD_DIM] = (qk_grad * HEAD_DIM ** (-0.5)).reshape(
            sources, per_peer, HEAD_DIM
        )
        results[:, place, HEAD_DIM:] = value_grad.reshape(sources, per_peer, HEAD_DIM)
        return carry

    lax.fori_loop(0, buckets, attend, 0, unroll=2)

    def scatter(source, carry):
        rows = results[source].astype(jnp.bfloat16)
        out_ref[source] = contract(slot_pick(slot_ref, source), rows, 0, 0).astype(jnp.bfloat16)
        return carry

    lax.fori_loop(0, sources, scatter, 0, unroll=2)


def kernel_call(body, out_shape, scratch_shapes, arguments):
    return pl.pallas_call(
        body,
        out_shape=out_shape,
        in_specs=[pl.BlockSpec(memory_space=pltpu.VMEM)] * len(arguments),
        out_specs=jax.tree.map(lambda _: pl.BlockSpec(memory_space=pltpu.VMEM), out_shape),
        scratch_shapes=scratch_shapes,
        compiler_params=pltpu.CompilerParams(vmem_limit_bytes=VMEM_BYTES),
    )(*arguments)


def head_owner_device(shared_qk, values, out_grad, out_weight, buckets):
    token_rows, row_width = shared_qk.shape
    heads = row_width // HEAD_DIM
    peers = lax.axis_size("ctx")
    per_peer = 2 * token_rows // peers
    half = token_rows // 2
    slots = peers * per_peer
    core = lax.axis_index("ctx") % 2
    first = core == 0
    partners = [(device, device ^ 1) for device in range(peers)]

    def exchange(block):
        return lax.ppermute(block, "ctx", partners)

    def swapped(block):
        return jnp.concatenate([block[:, half:], block[:, :half]], axis=1)

    def everywhere(block):
        return lax.all_to_all(block, "ctx", split_axis=0, concat_axis=0, tiled=True)

    def by_head(rows):
        return rows.reshape(2, half, heads, HEAD_DIM).transpose(2, 0, 1, 3)

    def by_token(blocks):
        return blocks.reshape(heads, 2, half, HEAD_DIM).transpose(1, 2, 0, 3).reshape(
            token_rows, row_width
        )

    whole_weight = lax.all_gather(out_weight, "ctx", axis=0, tiled=True)

    tag = jnp.pad(buckets.astype(jnp.bfloat16).reshape(1, -1), ((0, 7), (0, 0)))
    sent = jnp.concatenate([by_head(shared_qk), by_head(values)], axis=-1)
    sent = jnp.concatenate(
        [
            sent.reshape(peers, half, 2 * HEAD_DIM),
            jnp.broadcast_to(tag[None], (peers, 8, 2 * HEAD_DIM)),
        ],
        axis=1,
    )
    mine = everywhere(sent)
    other = exchange(mine[:, :half])

    all_buckets = mine[:, half].astype(jnp.int32).reshape(peers, 2, token_rows)
    own = jnp.where(first, all_buckets[:, 0], all_buckets[:, 1])
    order = jnp.arange(token_rows, dtype=jnp.int32)
    same = (own[:, :, None] == own[:, None, :]) & (order[None, :] < order[:, None])[None]
    position = jnp.sum(same.astype(jnp.int32), axis=2)
    slot = own * per_peer + position
    slot = jnp.where(first, slot, swapped(slot))
    bucket_ids = jnp.arange(peers, dtype=jnp.int32)
    counts = jnp.sum((own[:, :, None] == bucket_ids).astype(jnp.int32), axis=1)
    before = (bucket_ids[None, :] < bucket_ids[:, None]).astype(jnp.int32)
    starts = jnp.sum(before[:, :, None] * counts[None], axis=1)
    within = jnp.arange(per_peer, dtype=jnp.int32)
    live = within < counts[:, :, None]
    code = jnp.where(live, jnp.where(starts[:, :, None] + within >= SPAN, 2.0, 1.0), 0.0)
    code = code.astype(jnp.float32).transpose(1, 0, 2).reshape(peers, peers * per_peer)

    result, log_slots = kernel_call(
        forward_kernel,
        (
            jax.ShapeDtypeStruct((peers, token_rows, HEAD_DIM), jnp.bfloat16),
            jax.ShapeDtypeStruct((peers, peers * per_peer), jnp.float32),
        ),
        [
            pltpu.VMEM((peers, slots, 2 * HEAD_DIM), jnp.float32),
            pltpu.VMEM((peers, slots, HEAD_DIM), jnp.float32),
        ],
        (mine, other, slot, code),
    )

    late_grad, result, log_slots = lax.optimization_barrier((out_grad, result, log_slots))
    attended_grad = jnp.dot(late_grad, whole_weight, preferred_element_type=jnp.float32).astype(
        jnp.bfloat16
    )
    grad_mine = everywhere(by_head(attended_grad).reshape(peers, half, HEAD_DIM))
    grad_rows = jnp.concatenate([grad_mine, exchange(grad_mine)], axis=1).astype(jnp.float32)

    chosen = slot[:, :, None] == jnp.arange(slots, dtype=jnp.int32)
    log_by_source = log_slots.reshape(peers, peers, per_peer).transpose(1, 0, 2).reshape(peers, slots)
    log_own = jnp.sum(jnp.where(chosen, log_by_source[:, None, :], 0.0), axis=2)
    log_other = swapped(exchange(log_own))
    result_other = swapped(exchange(result))
    largest = jnp.maximum(log_own, log_other)
    lifted_own, lifted_other = jnp.exp(log_own - largest), jnp.exp(log_other - largest)
    lifted_sum = lifted_own + lifted_other
    weight_own, weight_other = lifted_own / lifted_sum, lifted_other / lifted_sum
    attended = (
        weight_own[:, :, None] * result.astype(jnp.float32)
        + weight_other[:, :, None] * result_other.astype(jnp.float32)
    ).astype(jnp.bfloat16)

    inner = jnp.sum(grad_rows * attended.astype(jnp.float32), axis=-1)
    shift = weight_own * inner
    query_grad = (weight_own[:, :, None] * grad_rows).astype(jnp.bfloat16)
    shift_slots = jnp.sum(jnp.where(chosen, shift[:, :, None], 0.0), axis=1)
    shift_slots = (
        shift_slots.reshape(peers, peers, per_peer).transpose(1, 0, 2).reshape(peers, slots)
    )

    attended_rows = by_token(everywhere(attended[:, :half]))

    grads = kernel_call(
        backward_kernel,
        jax.ShapeDtypeStruct((peers, token_rows, 2 * HEAD_DIM), jnp.bfloat16),
        [
            pltpu.VMEM((peers, slots, 3 * HEAD_DIM), jnp.float32),
            pltpu.VMEM((peers, slots, 2 * HEAD_DIM), jnp.float32),
        ],
        (mine, other, query_grad, slot, code, log_slots, shift_slots),
    )
    grads_other = exchange(grads[:, half:])
    total = (grads[:, :half].astype(jnp.float32) + grads_other.astype(jnp.float32)).astype(
        jnp.bfloat16
    )
    back = everywhere(total)
    grad_qk = by_token(back[:, :, :HEAD_DIM])
    grad_values = by_token(back[:, :, HEAD_DIM:])

    mixed = contract(attended_rows, whole_weight, 1, 1).astype(jnp.bfloat16)

    plane = peers // PLANES
    groups = [[level * plane + place for place in range(plane)] for level in range(PLANES)]
    plane_grad = lax.all_gather(out_grad, "ctx", axis=0, tiled=True, axis_index_groups=groups)
    plane_attended = lax.all_to_all(
        attended_rows, "ctx", split_axis=1, concat_axis=0, tiled=True, axis_index_groups=groups
    )
    partial = contract(plane_grad, plane_attended, 0, 0) * (1.0 / math.sqrt(token_rows * peers))
    shares = everywhere(
        partial.astype(jnp.bfloat16).reshape(peers, row_width // peers, row_width // plane)
    )
    shares = shares.reshape((PLANES, plane) + shares.shape[1:]).astype(jnp.float32)
    grad_weight = jnp.sum(shares, axis=0).transpose(1, 0, 2).reshape(-1, row_width)
    return (mixed, grad_qk, grad_values, grad_weight)


def per_device(shared_qk, values, out_grad, out_weight, buckets):
    token_rows, row_width = shared_qk.shape
    peers = lax.axis_size("ctx")
    fits = (
        lax.axis_size("head") == 1
        and buckets.shape[0] == 2
        and peers == 2 * (row_width // HEAD_DIM)
        and 2 * token_rows == TALL
        and TALL // peers == 8
    )
    whole = head_owner_device if fits else bucket_owner_device
    return whole(shared_qk, values, out_grad, out_weight, buckets)


def solution(mesh):
    in_specs = (
        P("ctx", "head"),
        P("ctx", "head"),
        P("ctx", "head"),
        P("ctx", "head"),
        P(None, "ctx"),
    )
    out_specs = (P("ctx", "head"), P("ctx", "head"), P("ctx", "head"), P("ctx", "head"))
    return jax.shard_map(
        per_device, mesh=mesh, in_specs=in_specs, out_specs=out_specs, check_vma=False
    )
```
